32 devices in a mesh: section: 2 (over x), dp: 4 (over y, core), mp: 4 (over z).
Axes of the slice: x: 2, y: 2, z: 4, core: 2. Of those that a mesh axis runs over, the one named last changes fastest.
Arguments:
- memory: bfloat16 [4, 256, 2048], P('dp', None, ('section', 'mp')), may hold values from -18 to 18
- key_weight: bfloat16 [2, 2048, 2048], P('section', None, 'mp'), may hold values from -1 to 1
- value_weight: bfloat16 [2, 2048, 2048], P('section', None, 'mp'), may hold values from -0.125 to 0.125
- queries: bfloat16 [2, 4, 256, 2048], P('section', 'dp', None, 'mp'), may hold values from -1024 to 1024
- cotangent: bfloat16 [2, 4, 256, 2048], P('section', 'dp', None, 'mp'), may hold values from -6 to 6
- target_lengths: int32 [4], P('dp'), may hold values from 64 to 256, as said below
Outputs:
- context: bfloat16 [2, 4, 256, 2048], P('section', 'dp', None, 'mp')
- mem_grad: float32 [4, 256, 2048], P('dp', None, ('section', 'mp'))
The draws below stay inside these ranges and needn't reach their ends.
Inputs may be any that keep to these rules, and one draw needn't show every extreme that they name: `target_lengths`: valid positions of a sequence come first; the last sequence is full.
All inputs are finite; a program needn't handle non-finite values.
Results may differ from the reference program's by a relative error of at most 0.013.
The reference program's roundings to bfloat16 on the way count: a program that leaves them out, or rounds other values in their place, can miss the bound.
Values may be sent and summed in bfloat16 or wider, within the bound.
A program may use at most 64 MiB of HBM per device.

```python
import math
import jax
import jax.numpy as jnp
from jax import lax

D = 2048
HEADS = 8
HEAD_DIM = 256
MEM = 256
TGT = 256
LAYERS = 2
SEQS = 4
HW = 2048


def shared_draws(key):
    memory_key = jax.random.fold_in(key, 101)
    weight_key = jax.random.fold_in(key, 102)
    memory = jax.random.truncated_normal(memory_key, -6.0, 6.0, (SEQS, MEM, D), jnp.float32)
    key_weight = jax.random.truncated_normal(weight_key, -4.0, 4.0, (LAYERS, D, HW), jnp.float32) / math.sqrt(D)
    return (memory, key_weight)


def draw_memory(key, part):
    return shared_draws(key)[0].astype(jnp.bfloat16)


def draw_key_weight(key, part):
    return shared_draws(key)[1].astype(jnp.bfloat16)


def draw_queries(key, part):
    base = jax.random.truncated_normal(jax.random.fold_in(key, 104), -6.0, 6.0, (LAYERS, SEQS, TGT, HW), jnp.float32) * 3.0
    return base.astype(jnp.bfloat16)


def draw_target_lengths(key, part):
    jitter = jax.random.randint(jax.random.fold_in(key, 108), (SEQS,), 0, TGT // 4 + 1)
    seq_index = jnp.arange(SEQS)
    rising = TGT // 4 + jitter + TGT // 2 * seq_index // (SEQS - 1)
    return jnp.where(seq_index == SEQS - 1, TGT, jnp.minimum(rising, TGT)).astype(jnp.int32)


def block_scale(key, shape, shards, least, top_value):
    gain = 1.0
    for axis_at, shards_of in shards:
        heights = jax.random.uniform(jax.random.fold_in(jax.random.fold_in(key, 6), axis_at), (shards_of,), jnp.float32, least / len(shards), top_value / len(shards))
        gain = gain * jnp.repeat(jnp.exp(heights), shape[axis_at] // shards_of).reshape((-1,) + (1,) * (len(shape) - 1 - axis_at))
    return gain


def bell_draw(own_key, extent, spread, reach, split=(), kind=jnp.bfloat16):
    values = spread * jax.random.normal(own_key, extent, jnp.float32)
    if split:
        values = values * block_scale(own_key, extent, split, -0.22, 0.18)
    return jnp.clip(values, -reach, reach).astype(kind)


def setup_inputs(seed: int = 0) -> dict:
    seeds = jax.random.split(jax.random.key(seed), 7)
    memory = draw_memory(jax.random.fold_in(seeds[6], 71), 0)
    key_weight = draw_key_weight(jax.random.fold_in(seeds[6], 71), 0)
    value_weight = bell_draw(seeds[2], (LAYERS, D, HW), D ** -0.5, 0.125, ((0, 2), (2, 4)))
    queries = draw_queries(jax.random.fold_in(seeds[6], 71), 0)
    cotangent = bell_draw(seeds[4], (LAYERS, SEQS, TGT, HW), 1.0, 6.0, ((0, 2), (1, 4), (3, 4)))
    target_lengths = draw_target_lengths(jax.random.fold_in(seeds[6], 71), 0)
    return {"memory": memory, "key_weight": key_weight, "value_weight": value_weight, "queries": queries, "cotangent": cotangent, "target_lengths": target_lengths}


def round_low(values_in):
    return lax.optimization_barrier(values_in.astype(jnp.bfloat16)).astype(jnp.float32)


def reference(memory, key_weight, value_weight, queries, cotangent, target_lengths):
    score_scale = HEAD_DIM ** -0.5
    lengths_float = target_lengths.astype(jnp.float32)
    loss_weight = jnp.float32(SEQS * TGT) / jnp.sum(lengths_float)
    valid = (jnp.arange(TGT, dtype=jnp.int32)[None, :] < target_lengths[:, None]).astype(jnp.float32)
    flat_memory = memory.reshape(SEQS * MEM, D)

    def layer_step(running, inputs):
        w_key, w_value, query_rows, cot_rows = inputs
        key_rows = jnp.dot(flat_memory, w_key, preferred_element_type=jnp.float32).astype(jnp.bfloat16)
        value_rows = jnp.dot(flat_memory, w_value, preferred_element_type=jnp.float32).astype(jnp.bfloat16)
        key_heads = key_rows.reshape(SEQS, MEM, HEADS, HEAD_DIM).astype(jnp.float32)
        value_heads = value_rows.reshape(SEQS, MEM, HEADS, HEAD_DIM).astype(jnp.float32)
        query_heads = query_rows.reshape(SEQS, TGT, HEADS, HEAD_DIM).astype(jnp.float32)
        scores = jnp.einsum('bthd,bshd->bhts', query_heads, key_heads) * score_scale
        attention = jax.nn.softmax(scores, axis=-1)
        attention_low = round_low(attention)
        context = jnp.einsum('bhts,bshd->bthd', attention_low, value_heads) * valid[:, :, None, None]
        context = context.astype(jnp.bfloat16)
        weighted = cot_rows.reshape(SEQS, TGT, HEADS, HEAD_DIM).astype(jnp.float32)
        weighted = round_low(weighted * (valid * loss_weight)[:, :, None, None])
        value_grad = jnp.einsum('bhts,bthd->bshd', attention_low, weighted).astype(jnp.bfloat16)
        prob_grad = jnp.einsum('bthd,bshd->bhts', weighted, value_heads)
        row_dot = jnp.sum(attention * prob_grad, axis=-1, keepdims=True)
        score_grad = round_low(attention * (prob_grad - row_dot) * score_scale)
        key_grad = jnp.einsum('bhts,bthd->bshd', score_grad, query_heads).astype(jnp.bfloat16)
        term = jnp.dot(key_grad.reshape(SEQS * MEM, HW), w_key.T, preferred_element_type=jnp.float32)
        term = term + jnp.dot(value_grad.reshape(SEQS * MEM, HW), w_value.T, preferred_element_type=jnp.float32)
        return running + term, context.reshape(SEQS, TGT, HW)

    start_grad = jnp.zeros((SEQS * MEM, D), jnp.float32)
    running, contexts = lax.scan(layer_step, start_grad, (key_weight, value_weight, queries, cotangent))
    return contexts, running.reshape(SEQS, MEM, D)
```

```python
import functools

import jax
import jax.numpy as jnp
from jax import lax
from jax.experimental import pallas as pl
from jax.experimental.pallas import tpu as pltpu
from jax.sharding import PartitionSpec as P

HEAD_DIM = 256
CHUNKS = 2
MESH = pl.DeviceIdType.MESH


def far_to_near(z, n):
    low, high, order = 0, n - 1, []
    for _ in range(n):
        take_low = (z - low) >= (high - z)
        order.append(jnp.where(take_low, low, high))
        low, high = jnp.where(take_low, low + 1, low), jnp.where(take_low, high, high - 1)
    return order


def fused_kernel(
    n, n_dp,
    len_ref, memory_ref, kw_ref, vw_ref, q_ref, cot_ref,
    ctx_out, grad_out,
    kw, vw, q, cot, mem_all, k_acc, v_acc, q_t, w, w_t, ctx, dk_t, dv_t,
    xs, xr, acc, zs, zr, len_own, len_all,
    local_sem, ag_own_send, ag_z_send, ag_x_send, ag_recv,
    rs_x_send, rs_x_recv, rs_z_send, rs_z_recv, len_send, len_recv,
):
    x = lax.axis_index("section")
    z = lax.axis_index("mp")
    dp = lax.axis_index("dp")
    other = 1 - x
    mem_rows, block = memory_ref.shape
    seq_rows, width = q_ref.shape
    heads = width // HEAD_DIM
    score_scale = HEAD_DIM ** (-0.5)
    part_rows = mem_rows // CHUNKS
    part_feats = block // CHUNKS
    far = far_to_near(z, n)
    near = far[::-1]

    own_slot = x * n + z
    loads = [
        pltpu.make_async_copy(src, dst, local_sem.at[i])
        for i, (src, dst) in enumerate(
            (
                (memory_ref, mem_all.at[own_slot]),
                (q_ref, q),
                (cot_ref, cot),
                (kw_ref, kw),
                (vw_ref, vw),
            )
        )
    ]
    for load in loads:
        load.start()
    length = len_ref[0]
    len_own[...] = jnp.full(len_own.shape, length.astype(jnp.float32), jnp.float32)

    barrier = pltpu.get_barrier_semaphore()
    pl.semaphore_signal(barrier, inc=1, device_id={"section": other}, device_id_type=MESH)
    for r in range(1, n_dp):
        peer = lax.rem(dp + r, n_dp)
        pl.semaphore_signal(barrier, inc=1, device_id={"dp": peer}, device_id_type=MESH)

    @pl.when(z > 0)
    def _():
        pl.semaphore_signal(barrier, inc=1, device_id={"mp": z - 1}, device_id_type=MESH)

    @pl.when(z < n - 1)
    def _():
        pl.semaphore_signal(barrier, inc=1, device_id={"mp": z + 1}, device_id_type=MESH)

    line_peers = jnp.where(z > 0, 1, 0) + jnp.where(z < n - 1, 1, 0)
    pl.semaphore_wait(barrier, n_dp + line_peers)

    def rows_of(c):
        return pl.ds(c * part_rows, part_rows)

    def send_block(src, slot, c, send_sem, device_id):
        return pltpu.make_async_remote_copy(
            src_ref=src,
            dst_ref=mem_all.at[slot, rows_of(c)],
            send_sem=send_sem,
            recv_sem=ag_recv.at[slot, c],
            device_id=device_id,
            device_id_type=MESH,
        )

    def own_to_left(c):
        return send_block(memory_ref.at[rows_of(c)], own_slot, c, ag_own_send.at[0, c], {"mp": z - 1})

    def own_to_right(c):
        return send_block(memory_ref.at[rows_of(c)], own_slot, c, ag_own_send.at[1, c], {"mp": z + 1})

    def to_x(k, c):
        slot = x * n + near[k]
        src = memory_ref.at[rows_of(c)] if k == 0 else mem_all.at[slot, rows_of(c)]
        return send_block(src, slot, c, ag_x_send.at[k, c], {"section": other})

    def relay(k, c):
        slot = x * n + near[k]
        dest = jnp.where(near[k] < z, z + 1, z - 1)
        return send_block(mem_all.at[slot, rows_of(c)], slot, c, ag_z_send.at[k, c], {"mp": dest})

    def relays(k):
        j = near[k]
        return ((j < z) & (z < n - 1)) | ((j > z) & (z > 0))

    def arrived(slot, c):
        send_block(mem_all.at[slot, rows_of(c)], slot, c, ag_x_send.at[0, c], {"section": other}).wait_recv()

    for c in range(CHUNKS):

        @pl.when(z > 0)
        def _():
            own_to_left(c).start()

        @pl.when(z < n - 1)
        def _():
            own_to_right(c).start()

        to_x(0, c).start()

    def send_length(r):
        peer = lax.rem(dp + r, n_dp)
        return pltpu.make_async_remote_copy(
            src_ref=len_own,
            dst_ref=len_all.at[dp],
            send_sem=len_send.at[r],
            recv_sem=len_recv.at[dp],
            device_id={"dp": peer},
            device_id_type=MESH,
        )

    for r in range(1, n_dp):
        send_length(r).start()

    def project(slot, first=False):
        rows = pl.ds(pl.multiple_of(slot * block, block), block)
        mem_block = mem_all[slot]
        k_part = jnp.dot(mem_block, kw[rows, :], preferred_element_type=jnp.float32)
        v_part = jnp.dot(mem_block, vw[rows, :], preferred_element_type=jnp.float32)
        if first:
            k_acc[...] = k_part
            v_acc[...] = v_part
        else:
            k_acc[...] += k_part
            v_acc[...] += v_part

    loads[0].wait()
    loads[1].wait()
    q_t[...] = q[...].T
    loads[2].wait()
    loads[3].wait()
    loads[4].wait()
    project(own_slot, first=True)

    valid = (
        lax.broadcasted_iota(jnp.int32, (seq_rows, 1), 0) < length
    ).astype(jnp.float32)
    for k in range(1, n):
        for c in range(CHUNKS):
            arrived(x * n + near[k], c)

            @pl.when(relays(k))
            def _():
                relay(k, c).start()

            to_x(k, c).start()
        if k == 1:
            total = len_own[...]
            for r in range(1, n_dp):
                peer = lax.rem(dp + r, n_dp)
                pltpu.make_async_remote_copy(
                    src_ref=len_own,
                    dst_ref=len_all.at[peer],
                    send_sem=len_send.at[r],
                    recv_sem=len_recv.at[peer],
                    device_id={"dp": peer},
                    device_id_type=MESH,
                ).wait_recv()
                total = total + len_all[peer]
            loss_weight = (float(n_dp * seq_rows) / total)[0:1, 0:1]
            weighted = (cot[...].astype(jnp.float32) * (valid * loss_weight)).astype(jnp.bfloat16)
            w[...] = weighted
            w_t[...] = weighted.T
        project(x * n + near[k])
        if k >= 2:
            for c in range(CHUNKS):
                arrived(other * n + near[k - 2], c)
            project(other * n + near[k - 2])
    for k in range(max(n - 2, 0), n):
        for c in range(CHUNKS):
            arrived(other * n + near[k], c)
        project(other * n + near[k])

    last = (((1,), (1,)), ((), ()))
    for h in range(heads):
        cols = slice(h * HEAD_DIM, (h + 1) * HEAD_DIM)
        key_h = k_acc[:, cols].astype(jnp.bfloat16)
        value_h = v_acc[:, cols].astype(jnp.bfloat16)
        scores = (
            lax.dot_general(q[:, cols], key_h, last, preferred_element_type=jnp.float32)
            * score_scale
        )
        prob_grad = lax.dot_general(w[:, cols], value_h, last, preferred_element_type=jnp.float32)
        top = jnp.max(scores, axis=-1, keepdims=True)
        powers = jnp.exp(scores - top)
        attention = powers / jnp.sum(powers, axis=-1, keepdims=True)
        attention_low = attention.astype(jnp.bfloat16)
        row_dot = jnp.sum(attention * prob_grad, axis=-1, keepdims=True)
        score_grad = (attention * (prob_grad - row_dot) * score_scale).astype(jnp.bfloat16)
        dv_t[cols, :] = jnp.dot(
            w_t[cols, :], attention_low, preferred_element_type=jnp.float32
        ).astype(jnp.bfloat16)
        dk_t[cols, :] = jnp.dot(
            q_t[cols, :], score_grad, preferred_element_type=jnp.float32
        ).astype(jnp.bfloat16)
        context = jnp.dot(attention_low, value_h, preferred_element_type=jnp.float32)
        ctx[:, cols] = (context * valid).astype(jnp.bfloat16)
    ctx_copy = pltpu.make_async_copy(ctx, ctx_out, local_sem.at[0])
    ctx_copy.start()

    def feats_of(c):
        return pl.ds(c * part_feats, part_feats)

    def grad_part(slot, c):
        rows = pl.ds(pl.multiple_of(slot * block + c * part_feats, part_feats), part_feats)
        return jnp.dot(
            kw[rows, :], dk_t[...], preferred_element_type=jnp.float32
        ) + jnp.dot(vw[rows, :], dv_t[...], preferred_element_type=jnp.float32)

    def sum_to_x(k, c):
        j = far[k]
        return pltpu.make_async_remote_copy(
            src_ref=xs.at[j, feats_of(c)],
            dst_ref=xr.at[j, feats_of(c)],
            send_sem=rs_x_send.at[k, c],
            recv_sem=rs_x_recv.at[j, c],
            device_id={"section": other},
            device_id_type=MESH,
        )

    def sum_along_z(k, c, slot):
        j = far[k]
        dest = jnp.where(j > z, z + 1, z - 1)
        return pltpu.make_async_remote_copy(
            src_ref=zs.at[j, feats_of(c)],
            dst_ref=zr.at[slot, feats_of(c)],
            send_sem=rs_z_send.at[k, c],
            recv_sem=rs_z_recv.at[slot, c],
            device_id={"mp": dest},
            device_id_type=MESH,
        )

    for k in range(n):
        for c in range(CHUNKS):
            xs[far[k], feats_of(c)] = grad_part(other * n + far[k], c).astype(jnp.bfloat16)
            sum_to_x(k, c).start()
    for k in range(n):
        for c in range(CHUNKS):
            acc[far[k], feats_of(c)] = grad_part(x * n + far[k], c)

    def target_slot(j):
        return jnp.where((j < z) & (z - 1 == j), n, j)

    for k in range(n - 1):
        j = far[k]
        has_source = ((j > z) & (z > 0)) | ((j < z) & (z < n - 1))
        for c in range(CHUNKS):
            sum_to_x(k, c).wait_recv()
            acc[j, feats_of(c)] += xr[j, feats_of(c)].astype(jnp.float32)

            @pl.when(has_source)
            def _():
                sum_along_z(k, c, j).wait_recv()
                acc[j, feats_of(c)] += zr[j, feats_of(c)].astype(jnp.float32)

            zs[j, feats_of(c)] = acc[j, feats_of(c)].astype(jnp.bfloat16)
            sum_along_z(k, c, target_slot(j)).start()

    for c in range(CHUNKS):
        sum_to_x(n - 1, c).wait_recv()
        grad_out[feats_of(c)] = acc[z, feats_of(c)] + xr[z, feats_of(c)].astype(jnp.float32)

        @pl.when(z > 0)
        def _():
            sum_along_z(0, c, z).wait_recv()
            grad_out[feats_of(c)] += zr[z, feats_of(c)].astype(jnp.float32)

        @pl.when(z < n - 1)
        def _():
            sum_along_z(0, c, n).wait_recv()
            grad_out[feats_of(c)] += zr[n, feats_of(c)].astype(jnp.float32)

    for c in range(CHUNKS):

        @pl.when(z > 0)
        def _():
            own_to_left(c).wait_send()

        @pl.when(z < n - 1)
        def _():
            own_to_right(c).wait_send()

        for k in range(n):
            to_x(k, c).wait_send()
            sum_to_x(k, c).wait_send()
        for k in range(1, n):

            @pl.when(relays(k))
            def _():
                relay(k, c).wait_send()

        for k in range(n - 1):
            sum_along_z(k, c, target_slot(far[k])).wait_send()
    for r in range(1, n_dp):
        send_length(r).wait_send()
    ctx_copy.wait()


def fused(n, n_dp, memory, key_weight, value_weight, queries, cotangent, target_lengths):
    mem_rows, block = memory.shape[1:]
    feats, width = key_weight.shape[1:]
    seq_rows = queries.shape[2]
    low, full = jnp.bfloat16, jnp.float32
    vmem, sem = pltpu.VMEM, pltpu.SemaphoreType.DMA
    anywhere = pl.BlockSpec(memory_space=pl.ANY)
    context, grad = pl.pallas_call(
        functools.partial(fused_kernel, n, n_dp),
        out_shape=(
            jax.ShapeDtypeStruct((seq_rows, width), low),
            jax.ShapeDtypeStruct((block, mem_rows), full),
        ),
        in_specs=[pl.BlockSpec(memory_space=pltpu.SMEM)] + [anywhere] * 5,
        out_specs=(anywhere, pl.BlockSpec(memory_space=pltpu.VMEM)),
        scratch_shapes=[
            vmem((feats, width), low),
            vmem((feats, width), low),
            vmem((seq_rows, width), low),
            vmem((seq_rows, width), low),
            vmem((2 * n, mem_rows, block), low),
            vmem((mem_rows, width), full),
            vmem((mem_rows, width), full),
            vmem((width, seq_rows), low),
            vmem((seq_rows, width), low),
            vmem((width, seq_rows), low),
            vmem((seq_rows, width), low),
            vmem((width, mem_rows), low),
            vmem((width, mem_rows), low),
            vmem((n, block, mem_rows), low),
            vmem((n, block, mem_rows), low),
            vmem((n, block, mem_rows), full),
            vmem((n, block, mem_rows), low),
            vmem((n + 1, block, mem_rows), low),
            vmem((8, 128), full),
            vmem((n_dp, 8, 128), full),
            sem((5,)),
            sem((2, CHUNKS)),
            sem((n, CHUNKS)),
            sem((n, CHUNKS)),
            sem((2 * n, CHUNKS)),
            sem((n, CHUNKS)),
            sem((n, CHUNKS)),
            sem((n, CHUNKS)),
            sem((n + 1, CHUNKS)),
            sem((n_dp,)),
            sem((n_dp,)),
        ],
        compiler_params=pltpu.CompilerParams(
            collective_id=0, has_side_effects=True, vmem_limit_bytes=60 * 1024 * 1024
        ),
    )(
        target_lengths,
        memory[0],
        key_weight[0],
        value_weight[0],
        queries[0, 0],
        cotangent[0, 0],
    )
    return context[None, None], grad.T[None]


def on_device(memory, key_weight, value_weight, queries, cotangent, target_lengths):
    width = key_weight.shape[2]
    head_count = width // HEAD_DIM
    seq_rows = queries.shape[2]
    score_scale = HEAD_DIM ** (-0.5)
    mem_block = memory[0]
    mem_rows = mem_block.shape[0]
    full_memory = lax.all_gather(mem_block, ("section", "mp"), axis=1, tiled=True)
    token_total = lax.psum(target_lengths.astype(jnp.float32), "dp")
    slot_total = float(lax.axis_size("dp") * target_lengths.shape[0] * seq_rows)
    loss_weight = slot_total / token_total[0]
    valid = (jnp.arange(seq_rows, dtype=jnp.int32) < target_lengths[0]).astype(jnp.float32)
    layer_index = 0
    key_rows = jnp.dot(
        full_memory, key_weight[layer_index], preferred_element_type=jnp.float32
    ).astype(jnp.bfloat16)
    value_rows = jnp.dot(
        full_memory, value_weight[layer_index], preferred_element_type=jnp.float32
    ).astype(jnp.bfloat16)
    key_heads = key_rows.reshape(mem_rows, head_count, HEAD_DIM)
    value_heads = value_rows.reshape(mem_rows, head_count, HEAD_DIM)
    query_heads = queries[layer_index, 0].reshape(seq_rows, head_count, HEAD_DIM)
    scores = (
        jnp.einsum("thd,shd->hts", query_heads, key_heads, preferred_element_type=jnp.float32)
        * score_scale
    )
    attention = jax.nn.softmax(scores, axis=-1)
    attention_low = attention.astype(jnp.bfloat16)
    context = jnp.einsum(
        "hts,shd->thd", attention_low, value_heads, preferred_element_type=jnp.float32
    )
    context = (context * valid[:, None, None]).astype(jnp.bfloat16)
    contexts = [context.reshape(seq_rows, width)]
    weighted = cotangent[layer_index, 0].astype(jnp.float32) * (valid * loss_weight)[:, None]
    weighted = weighted.astype(jnp.bfloat16).reshape(seq_rows, head_count, HEAD_DIM)
    value_grad = jnp.einsum(
        "hts,thd->shd", attention_low, weighted, preferred_element_type=jnp.float32
    )
    value_grads = [value_grad.astype(jnp.bfloat16).reshape(mem_rows, width)]
    prob_grad = jnp.einsum(
        "thd,shd->hts", weighted, value_heads, preferred_element_type=jnp.float32
    )
    row_dot = jnp.sum(attention * prob_grad, axis=-1, keepdims=True)
    score_grad = (attention * (prob_grad - row_dot) * score_scale).astype(jnp.bfloat16)
    key_grad = jnp.einsum(
        "hts,thd->shd", score_grad, query_heads, preferred_element_type=jnp.float32
    )
    key_grads = [key_grad.astype(jnp.bfloat16).reshape(mem_rows, width)]
    contract_last = (((1,), (1,)), ((), ()))
    layer_index = 0
    key_part = key_weight[layer_index]
    value_part = value_weight[layer_index]
    running = lax.dot_general(
        key_part, key_grads[layer_index], contract_last, preferred_element_type=jnp.float32
    )
    running = running + lax.dot_general(
        value_part, value_grads[layer_index], contract_last, preferred_element_type=jnp.float32
    )
    section_part = lax.psum_scatter(
        running.astype(jnp.bfloat16), "section", scatter_dimension=0, tiled=True
    )
    own_part = lax.psum_scatter(section_part, "mp", scatter_dimension=0, tiled=True).astype(
        jnp.float32
    )
    own_grad = own_part.T
    context_out = jnp.stack(contexts, axis=0)[:, None]
    return (context_out, own_grad[None])


def solution(mesh):
    sections, n, n_dp = mesh.shape["section"], mesh.shape["mp"], mesh.shape["dp"]

    def per_device(memory, key_weight, value_weight, queries, cotangent, target_lengths):
        args = (memory, key_weight, value_weight, queries, cotangent, target_lengths)
        part = 128 * CHUNKS
        if sections == 2 and memory.shape[2] % part == 0 and memory.shape[1] % part == 0:
            return fused(n, n_dp, *args)
        return on_device(*args)

    return jax.shard_map(
        per_device,
        mesh=mesh,
        in_specs=(
            P("dp", None, ("section", "mp")),
            P("section", None, "mp"),
            P("section", None, "mp"),
            P("section", "dp", None, "mp"),
            P("section", "dp", None, "mp"),
            P("dp"),
        ),
        out_specs=(P("section", "dp", None, "mp"), P("dp", None, ("section", "mp"))),
        check_vma=False,
    )
```

```python
import functools

import jax
import jax.numpy as jnp
from jax import lax
from jax.experimental import pallas as pl
from jax.experimental.pallas import tpu as pltpu
from jax.sharding import PartitionSpec as P

HEAD_DIM = 256
CHUNKS = 4
HALF = CHUNKS // 2
MESH = pl.DeviceIdType.MESH


def far_to_near(z, n):
    low, high, order = 0, n - 1, []
    for _ in range(n):
        take_low = (z - low) >= (high - z)
        order.append(jnp.where(take_low, low, high))
        low, high = jnp.where(take_low, low + 1, low), jnp.where(take_low, high, high - 1)
    return order


def finish_kernel(ctx_ref, grad_ref, ctx_out, grad_out, grad, grad_t, sems):
    ctx_copy = pltpu.make_async_copy(ctx_ref, ctx_out, sems.at[0])
    load = pltpu.make_async_copy(grad_ref, grad, sems.at[1])
    load.start()
    ctx_copy.start()
    load.wait()
    grad_t[...] = grad[...].T
    store = pltpu.make_async_copy(grad_t, grad_out, sems.at[1])
    store.start()
    ctx_copy.wait()
    store.wait()


def fused_kernel(
    n, n_dp,
    len_ref, memory_ref, kw_ref, vw_ref, q_ref, cot_ref,
    ctx_out, grad_out,
    kw, vw, q, cot, mem_all, k_acc, v_acc, q_t, w, w_t, ctx, dk_t, dv_t,
    xs, xr, acc, zs, zr, hs, hr, len_own, len_all,
    local_sem, ag_own_send, ag_z_send, ag_x_send, ag_recv,
    rs_x_send, rs_x_recv, rs_z_send, rs_z_recv, half_ag_send, half_rs_send, half_rs_recv, len_send, len_recv,
):
    x = lax.axis_index("section")
    z = lax.axis_index("mp")
    dp = lax.axis_index("dp")
    other = 1 - x
    mem_rows, block = memory_ref.shape
    seq_rows, width = q_ref.shape
    heads = width // HEAD_DIM
    score_scale = HEAD_DIM ** (-0.5)
    part_rows = mem_rows // CHUNKS
    part_feats = block // CHUNKS
    far = far_to_near(z, n)
    near = far[::-1]
    pair = z + 1 - 2 * lax.rem(z, 2)
    seen, other_order = False, []
    for k in range(n - 1):
        seen = seen | (near[k] == pair)
        other_order.append(jnp.where(seen, near[k + 1], near[k]))
    other_order.append(pair)

    own_slot = x * n + z
    loads = [
        pltpu.make_async_copy(src, dst, local_sem.at[i])
        for i, (src, dst) in enumerate(
            (
                (memory_ref, mem_all.at[own_slot]),
                (q_ref, q),
                (cot_ref, cot),
                (kw_ref, kw),
                (vw_ref, vw),
            )
        )
    ]
    for load in loads:
        load.start()
    length = len_ref[0]
    len_own[...] = jnp.full(len_own.shape, length.astype(jnp.float32), jnp.float32)

    barrier = pltpu.get_barrier_semaphore()
    pl.semaphore_signal(barrier, inc=1, device_id={"section": other}, device_id_type=MESH)
    for r in range(1, n_dp):
        peer = lax.rem(dp + r, n_dp)
        pl.semaphore_signal(barrier, inc=1, device_id={"dp": peer}, device_id_type=MESH)

    @pl.when(z > 0)
    def _():
        pl.semaphore_signal(barrier, inc=1, device_id={"mp": z - 1}, device_id_type=MESH)

    @pl.when(z < n - 1)
    def _():
        pl.semaphore_signal(barrier, inc=1, device_id={"mp": z + 1}, device_id_type=MESH)

    line_peers = jnp.where(z > 0, 1, 0) + jnp.where(z < n - 1, 1, 0)
    pl.semaphore_wait(barrier, n_dp + line_peers)

    def rows_of(c):
        return pl.ds(c * part_rows, part_rows)

    def send_block(src, slot, c, send_sem, device_id):
        return pltpu.make_async_remote_copy(
            src_ref=src,
            dst_ref=mem_all.at[slot, rows_of(c)],
            send_sem=send_sem,
            recv_sem=ag_recv.at[slot, c],
            device_id=device_id,
            device_id_type=MESH,
        )

    def own_to_left(c):
        return send_block(memory_ref.at[rows_of(c)], own_slot, c, ag_own_send.at[0, c], {"mp": z - 1})

    def own_to_right(c):
        return send_block(memory_ref.at[rows_of(c)], own_slot, c, ag_own_send.at[1, c], {"mp": z + 1})

    def to_x(k, c):
        slot = x * n + near[k]
        src = memory_ref.at[rows_of(c)] if k == 0 else mem_all.at[slot, rows_of(c)]
        return send_block(src, slot, c, ag_x_send.at[k, c], {"section": other})

    def relay(k, c):
        slot = x * n + near[k]
        dest = jnp.where(near[k] < z, z + 1, z - 1)
        return send_block(mem_all.at[slot, rows_of(c)], slot, c, ag_z_send.at[k, c], {"mp": dest})

    def relays(k):
        j = near[k]
        return ((j < z) & (z < n - 1)) | ((j > z) & (z > 0))

    def arrived(slot, c):
        send_block(mem_all.at[slot, rows_of(c)], slot, c, ag_x_send.at[0, c], {"section": other}).wait_recv()

    for c in range(CHUNKS):

        @pl.when(z > 0)
        def _():
            own_to_left(c).start()

        @pl.when(z < n - 1)
        def _():
            own_to_right(c).start()

        to_x(0, c).start()

    def send_length(r):
        peer = lax.rem(dp + r, n_dp)
        return pltpu.make_async_remote_copy(
            src_ref=len_own,
            dst_ref=len_all.at[dp],
            send_sem=len_send.at[r],
            recv_sem=len_recv.at[dp],
            device_id={"dp": peer},
            device_id_type=MESH,
        )

    for r in range(1, n_dp):
        send_length(r).start()

    def half_to_pair(c):
        slot = other * n + z
        return send_block(
            mem_all.at[slot, rows_of(c)], slot, c, half_ag_send.at[c], {"mp": pair}
        )

    def start_to_x(k, c):
        if c < HALF:
            to_x(k, c).start()
        else:

            @pl.when(near[k] != pair)
            def _():
                to_x(k, c).start()

    def project(slot, first=False):
        rows = pl.ds(pl.multiple_of(slot * block, block), block)
        mem_block = mem_all[slot]
        k_part = jnp.dot(mem_block, kw[rows, :], preferred_element_type=jnp.float32)
        v_part = jnp.dot(mem_block, vw[rows, :], preferred_element_type=jnp.float32)
        if first:
            k_acc[...] = k_part
            v_acc[...] = v_part
        else:
            k_acc[...] += k_part
            v_acc[...] += v_part

    loads[0].wait()
    loads[1].wait()
    q_t[...] = q[...].T
    loads[2].wait()
    loads[3].wait()
    loads[4].wait()
    project(own_slot, first=True)

    valid = (
        lax.broadcasted_iota(jnp.int32, (seq_rows, 1), 0) < length
    ).astype(jnp.float32)
    for k in range(1, n):
        for c in range(CHUNKS):
            arrived(x * n + near[k], c)

            @pl.when(relays(k))
            def _():
                relay(k, c).start()

            start_to_x(k, c)
        if k == 1:
            total = len_own[...]
            for r in range(1, n_dp):
                peer = lax.rem(dp + r, n_dp)
                pltpu.make_async_remote_copy(
                    src_ref=len_own,
                    dst_ref=len_all.at[peer],
                    send_sem=len_send.at[r],
                    recv_sem=len_recv.at[peer],
                    device_id={"dp": peer},
                    device_id_type=MESH,
                ).wait_recv()
                total = total + len_all[peer]
            loss_weight = (float(n_dp * seq_rows) / total)[0:1, 0:1]
            weighted = (cot[...].astype(jnp.float32) * (valid * loss_weight)).astype(jnp.bfloat16)
            w[...] = weighted
            w_t[...] = weighted.T
        if k == n - 1:
            for c in range(HALF, CHUNKS):
                half_to_pair(c).start()
        project(x * n + near[k])
        if k >= 2:
            for c in range(CHUNKS):
                arrived(other * n + other_order[k - 2], c)
            project(other * n + other_order[k - 2])
    for k in range(n - 2, n):
        for c in range(CHUNKS):
            arrived(other * n + other_order[k], c)
        project(other * n + other_order[k])

    last = (((1,), (1,)), ((), ()))
    for h in range(heads):
        cols = slice(h * HEAD_DIM, (h + 1) * HEAD_DIM)
        key_h = k_acc[:, cols].astype(jnp.bfloat16)
        value_h = v_acc[:, cols].astype(jnp.bfloat16)
        scores = (
            lax.dot_general(q[:, cols], key_h, last, preferred_element_type=jnp.float32)
            * score_scale
        )
        prob_grad = lax.dot_general(w[:, cols], value_h, last, preferred_element_type=jnp.float32)
        top = jnp.max(scores, axis=-1, keepdims=True)
        powers = jnp.exp(scores - top)
        attention = powers / jnp.sum(powers, axis=-1, keepdims=True)
        attention_low = attention.astype(jnp.bfloat16)
        row_dot = jnp.sum(attention * prob_grad, axis=-1, keepdims=True)
        score_grad = (attention * (prob_grad - row_dot) * score_scale).astype(jnp.bfloat16)
        dv_t[cols, :] = jnp.dot(
            w_t[cols, :], attention_low, preferred_element_type=jnp.float32
        ).astype(jnp.bfloat16)
        dk_t[cols, :] = jnp.dot(
            q_t[cols, :], score_grad, preferred_element_type=jnp.float32
        ).astype(jnp.bfloat16)
        context = jnp.dot(attention_low, value_h, preferred_element_type=jnp.float32)
        ctx[:, cols] = (context * valid).astype(jnp.bfloat16)
    ctx_copy = pltpu.make_async_copy(ctx, ctx_out, local_sem.at[0])
    ctx_copy.start()

    def feats_of(c):
        return pl.ds(c * part_feats, part_feats)

    half_feats = block // 2

    def half_of(i):
        return pl.ds(i * half_feats, half_feats)

    def grad_part(slot, i):
        rows = pl.ds(pl.multiple_of(slot * block + i * half_feats, half_feats), half_feats)
        return jnp.dot(
            kw[rows, :], dk_t[...], preferred_element_type=jnp.float32
        ) + jnp.dot(vw[rows, :], dv_t[...], preferred_element_type=jnp.float32)

    def sum_to_x(k, c):
        j = far[k]
        return pltpu.make_async_remote_copy(
            src_ref=xs.at[j, feats_of(c)],
            dst_ref=xr.at[j, feats_of(c)],
            send_sem=rs_x_send.at[k, c],
            recv_sem=rs_x_recv.at[j, c],
            device_id={"section": other},
            device_id_type=MESH,
        )

    def sum_along_z(k, c, slot):
        j = far[k]
        dest = jnp.where(j > z, z + 1, z - 1)
        return pltpu.make_async_remote_copy(
            src_ref=zs.at[j, feats_of(c)],
            dst_ref=zr.at[slot, feats_of(c)],
            send_sem=rs_z_send.at[k, c],
            recv_sem=rs_z_recv.at[slot, c],
            device_id={"mp": dest},
            device_id_type=MESH,
        )

    def sum_to_pair(c):
        rows = pl.ds((c - HALF) * part_feats, part_feats)
        return pltpu.make_async_remote_copy(
            src_ref=hs.at[rows],
            dst_ref=hr.at[rows],
            send_sem=half_rs_send.at[c],
            recv_sem=half_rs_recv.at[c],
            device_id={"mp": pair},
            device_id_type=MESH,
        )

    for k in range(n):
        j = far[k]
        xs[j, half_of(0)] = grad_part(other * n + j, 0).astype(jnp.bfloat16)
        for c in range(HALF):
            sum_to_x(k, c).start()
        if k == n - 1:
            tail = grad_part(other * n + j, 1)
            for c in range(HALF, CHUNKS):
                sum_to_pair(c).wait_recv()
            xs[j, half_of(1)] = (tail + hr[...].astype(jnp.float32)).astype(jnp.bfloat16)
            for c in range(HALF, CHUNKS):
                sum_to_x(k, c).start()
        else:

            @pl.when(j != pair)
            def _():
                xs[j, half_of(1)] = grad_part(other * n + j, 1).astype(jnp.bfloat16)
                for c in range(HALF, CHUNKS):
                    sum_to_x(k, c).start()

        if k == 0:
            hs[...] = grad_part(other * n + pair, 1).astype(jnp.bfloat16)
            for c in range(HALF, CHUNKS):
                sum_to_pair(c).start()
    for k in range(n):
        for i in range(2):
            acc[far[k], half_of(i)] = grad_part(x * n + far[k], i)

    def target_slot(j):
        return jnp.where((j < z) & (z - 1 == j), n, j)

    for k in range(n - 1):
        j = far[k]
        has_source = ((j > z) & (z > 0)) | ((j < z) & (z < n - 1))
        for c in range(CHUNKS):

            @pl.when((j != pair) | (c < HALF))
            def _():
                sum_to_x(k, c).wait_recv()
                acc[j, feats_of(c)] += xr[j, feats_of(c)].astype(jnp.float32)

            @pl.when(has_source)
            def _():
                sum_along_z(k, c, j).wait_recv()
                acc[j, feats_of(c)] += zr[j, feats_of(c)].astype(jnp.float32)

            zs[j, feats_of(c)] = acc[j, feats_of(c)].astype(jnp.bfloat16)
            sum_along_z(k, c, target_slot(j)).start()

    for c in range(CHUNKS):
        sum_to_x(n - 1, c).wait_recv()
        grad_out[feats_of(c)] = acc[z, feats_of(c)] + xr[z, feats_of(c)].astype(jnp.float32)

        @pl.when(z > 0)
        def _():
            sum_along_z(0, c, z).wait_recv()
            grad_out[feats_of(c)] += zr[z, feats_of(c)].astype(jnp.float32)

        @pl.when(z < n - 1)
        def _():
            sum_along_z(0, c, n).wait_recv()
            grad_out[feats_of(c)] += zr[n, feats_of(c)].astype(jnp.float32)

    for c in range(CHUNKS):

        @pl.when(z > 0)
        def _():
            own_to_left(c).wait_send()

        @pl.when(z < n - 1)
        def _():
            own_to_right(c).wait_send()

        for k in range(n):

            @pl.when((near[k] != pair) | (c < HALF))
            def _():
                to_x(k, c).wait_send()

            @pl.when((far[k] != pair) | (c < HALF))
            def _():
                sum_to_x(k, c).wait_send()

        if c >= HALF:
            half_to_pair(c).wait_send()
            sum_to_pair(c).wait_send()
        for k in range(1, n):

            @pl.when(relays(k))
            def _():
                relay(k, c).wait_send()

        for k in range(n - 1):
            sum_along_z(k, c, target_slot(far[k])).wait_send()
    for r in range(1, n_dp):
        send_length(r).wait_send()
    ctx_copy.wait()


def fused(n, n_dp, memory, key_weight, value_weight, queries, cotangent, target_lengths):
    mem_rows, block = memory.shape[1:]
    feats, width = key_weight.shape[1:]
    seq_rows = queries.shape[2]
    low, full = jnp.bfloat16, jnp.float32
    vmem, sem = pltpu.VMEM, pltpu.SemaphoreType.DMA
    anywhere = pl.BlockSpec(memory_space=pl.ANY)
    context, grad = pl.pallas_call(
        functools.partial(fused_kernel, n, n_dp),
        out_shape=(
            jax.ShapeDtypeStruct((seq_rows, width), low),
            jax.ShapeDtypeStruct((block, mem_rows), full),
        ),
        in_specs=[pl.BlockSpec(memory_space=pltpu.SMEM)] + [anywhere] * 5,
        out_specs=(anywhere, pl.BlockSpec(memory_space=pltpu.VMEM)),
        scratch_shapes=[
            vmem((feats, width), low),
            vmem((feats, width), low),
            vmem((seq_rows, width), low),
            vmem((seq_rows, width), low),
            vmem((2 * n, mem_rows, block), low),
            vmem((mem_rows, width), full),
            vmem((mem_rows, width), full),
            vmem((width, seq_rows), low),
            vmem((seq_rows, width), low),
            vmem((width, seq_rows), low),
            vmem((seq_rows, width), low),
            vmem((width, mem_rows), low),
            vmem((width, mem_rows), low),
            vmem((n, block, mem_rows), low),
            vmem((n, block, mem_rows), low),
            vmem((n, block, mem_rows), full),
            vmem((n, block, mem_rows), low),
            vmem((n + 1, block, mem_rows), low),
            vmem((block // 2, mem_rows), low),
            vmem((block // 2, mem_rows), low),
            vmem((8, 128), full),
            vmem((n_dp, 8, 128), full),
            sem((5,)),
            sem((2, CHUNKS)),
            sem((n, CHUNKS)),
            sem((n, CHUNKS)),
            sem((2 * n, CHUNKS)),
            sem((n, CHUNKS)),
            sem((n, CHUNKS)),
            sem((n, CHUNKS)),
            sem((n + 1, CHUNKS)),
            sem((CHUNKS,)),
            sem((CHUNKS,)),
            sem((CHUNKS,)),
            sem((n_dp,)),
            sem((n_dp,)),
        ],
        compiler_params=pltpu.CompilerParams(
            collective_id=0, has_side_effects=True, vmem_limit_bytes=60 * 1024 * 1024
        ),
    )(
        target_lengths,
        memory[0],
        key_weight[0],
        value_weight[0],
        queries[0, 0],
        cotangent[0, 0],
    )
    context, grad = pl.pallas_call(
        finish_kernel,
        out_shape=(
            jax.ShapeDtypeStruct((seq_rows, width), low),
            jax.ShapeDtypeStruct((mem_rows, block), full),
        ),
        in_specs=[anywhere] * 2,
        out_specs=(anywhere, anywhere),
        scratch_shapes=[vmem((block, mem_rows), full), vmem((mem_rows, block), full), sem((2,))],
        compiler_params=pltpu.CompilerParams(vmem_limit_bytes=60 * 1024 * 1024),
    )(context, grad)
    return context[None, None], grad[None]


def on_device(memory, key_weight, value_weight, queries, cotangent, target_lengths):
    width = key_weight.shape[2]
    head_count = width // HEAD_DIM
    seq_rows = queries.shape[2]
    score_scale = HEAD_DIM ** (-0.5)
    mem_block = memory[0]
    mem_rows = mem_block.shape[0]
    full_memory = lax.all_gather(mem_block, ("section", "mp"), axis=1, tiled=True)
    token_total = lax.psum(target_lengths.astype(jnp.float32), "dp")
    slot_total = float(lax.axis_size("dp") * target_lengths.shape[0] * seq_rows)
    loss_weight = slot_total / token_total[0]
    valid = (jnp.arange(seq_rows, dtype=jnp.int32) < target_lengths[0]).astype(jnp.float32)
    layer_index = 0
    key_rows = jnp.dot(
        full_memory, key_weight[layer_index], preferred_element_type=jnp.float32
    ).astype(jnp.bfloat16)
    value_rows = jnp.dot(
        full_memory, value_weight[layer_index], preferred_element_type=jnp.float32
    ).astype(jnp.bfloat16)
    key_heads = key_rows.reshape(mem_rows, head_count, HEAD_DIM)
    value_heads = value_rows.reshape(mem_rows, head_count, HEAD_DIM)
    query_heads = queries[layer_index, 0].reshape(seq_rows, head_count, HEAD_DIM)
    scores = (
        jnp.einsum("thd,shd->hts", query_heads, key_heads, preferred_element_type=jnp.float32)
        * score_scale
    )
    attention = jax.nn.softmax(scores, axis=-1)
    attention_low = attention.astype(jnp.bfloat16)
    context = jnp.einsum(
        "hts,shd->thd", attention_low, value_heads, preferred_element_type=jnp.float32
    )
    context = (context * valid[:, None, None]).astype(jnp.bfloat16)
    contexts = [context.reshape(seq_rows, width)]
    weighted = cotangent[layer_index, 0].astype(jnp.float32) * (valid * loss_weight)[:, None]
    weighted = weighted.astype(jnp.bfloat16).reshape(seq_rows, head_count, HEAD_DIM)
    value_grad = jnp.einsum(
        "hts,thd->shd", attention_low, weighted, preferred_element_type=jnp.float32
    )
    value_grads = [value_grad.astype(jnp.bfloat16).reshape(mem_rows, width)]
    prob_grad = jnp.einsum(
        "thd,shd->hts", weighted, value_heads, preferred_element_type=jnp.float32
    )
    row_dot = jnp.sum(attention * prob_grad, axis=-1, keepdims=True)
    score_grad = (attention * (prob_grad - row_dot) * score_scale).astype(jnp.bfloat16)
    key_grad = jnp.einsum(
        "hts,thd->shd", score_grad, query_heads, preferred_element_type=jnp.float32
    )
    key_grads = [key_grad.astype(jnp.bfloat16).reshape(mem_rows, width)]
    contract_last = (((1,), (1,)), ((), ()))
    layer_index = 0
    key_part = key_weight[layer_index]
    value_part = value_weight[layer_index]
    running = lax.dot_general(
        key_part, key_grads[layer_index], contract_last, preferred_element_type=jnp.float32
    )
    running = running + lax.dot_general(
        value_part, value_grads[layer_index], contract_last, preferred_element_type=jnp.float32
    )
    section_part = lax.psum_scatter(
        running.astype(jnp.bfloat16), "section", scatter_dimension=0, tiled=True
    )
    own_part = lax.psum_scatter(section_part, "mp", scatter_dimension=0, tiled=True).astype(
        jnp.float32
    )
    own_grad = own_part.T
    context_out = jnp.stack(contexts, axis=0)[:, None]
    return (context_out, own_grad[None])


def solution(mesh):
    sections, n, n_dp = mesh.shape["section"], mesh.shape["mp"], mesh.shape["dp"]

    def per_device(memory, key_weight, value_weight, queries, cotangent, target_lengths):
        args = (memory, key_weight, value_weight, queries, cotangent, target_lengths)
        mem_rows, block = memory.shape[1:]
        if sections == 2 and n >= 4 and n % 2 == 0 and mem_rows % 128 == 0 and block % 128 == 0:
            return fused(n, n_dp, *args)
        return on_device(*args)

    return jax.shard_map(
        per_device,
        mesh=mesh,
        in_specs=(
            P("dp", None, ("section", "mp")),
            P("section", None, "mp"),
            P("section", None, "mp"),
            P("section", "dp", None, "mp"),
            P("section", "dp", None, "mp"),
            P("dp"),
        ),
        out_specs=(P("section", "dp", None, "mp"), P("dp", None, ("section", "mp"))),
        check_vma=False,
    )
```

```python
import functools

import jax
import jax.numpy as jnp
from jax import lax
from jax.experimental import pallas as pl
from jax.experimental.pallas import tpu as pltpu
from jax.sharding import PartitionSpec as P

HEAD_DIM = 256
CHUNKS = 2
MESH = pl.DeviceIdType.MESH


def far_to_near(z, n):
    low, high, order = 0, n - 1, []
    for _ in range(n):
        take_low = (z - low) >= (high - z)
        order.append(jnp.where(take_low, low, high))
        low, high = jnp.where(take_low, low + 1, low), jnp.where(take_low, high, high - 1)
    return order


def pick(order, at):
    found = order[0]
    for i in range(1, len(order)):
        found = jnp.where(at == i, order[i], found)
    return found


def finish_kernel(ctx_ref, grad_ref, ctx_out, grad_out, ctx, grad, grad_t, sems):
    grad_load = pltpu.make_async_copy(grad_ref, grad, sems.at[0])
    ctx_load = pltpu.make_async_copy(ctx_ref, ctx, sems.at[1])
    grad_load.start()
    ctx_load.start()
    grad_load.wait()
    grad_t[...] = grad[...].T
    grad_store = pltpu.make_async_copy(grad_t, grad_out, sems.at[2])
    grad_store.start()
    ctx_load.wait()
    ctx_store = pltpu.make_async_copy(ctx, ctx_out, sems.at[3])
    ctx_store.start()
    grad_store.wait()
    ctx_store.wait()


def fused_kernel(
    n, n_dp,
    len_ref, memory_ref, kw_ref, vw_ref, q_ref, cot_ref,
    ctx_out, grad_out,
    kw, vw, q, cot, mem_all, k_acc, v_acc, q_t, w, w_t, ctx, dk_t, dv_t,
    xs, xr, acc, zs, zr, len_own, len_all,
    local_sem, ag_own_send, ag_z_send, ag_x_send, ag_recv,
    rs_x_send, rs_x_recv, rs_z_send, rs_z_recv, len_send, len_recv,
):
    x = lax.axis_index("section")
    z = lax.axis_index("mp")
    dp = lax.axis_index("dp")
    other = 1 - x
    mem_rows, block = memory_ref.shape
    seq_rows, width = q_ref.shape
    heads = width // HEAD_DIM
    score_scale = HEAD_DIM ** (-0.5)
    part_rows = mem_rows // CHUNKS
    part_feats = block // CHUNKS
    far = far_to_near(z, n)
    near = far[::-1]

    own_slot = x * n + z
    loads = [
        pltpu.make_async_copy(src, dst, local_sem.at[i])
        for i, (src, dst) in enumerate(
            (
                (memory_ref, mem_all.at[own_slot]),
                (q_ref, q),
                (cot_ref, cot),
                (kw_ref, kw),
                (vw_ref, vw),
            )
        )
    ]
    for load in loads:
        load.start()
    length = len_ref[0]
    len_own[...] = jnp.full(len_own.shape, length.astype(jnp.float32), jnp.float32)

    barrier = pltpu.get_barrier_semaphore()
    pl.semaphore_signal(barrier, inc=1, device_id={"section": other}, device_id_type=MESH)
    for r in range(1, n_dp):
        peer = lax.rem(dp + r, n_dp)
        pl.semaphore_signal(barrier, inc=1, device_id={"dp": peer}, device_id_type=MESH)

    @pl.when(z > 0)
    def _():
        pl.semaphore_signal(barrier, inc=1, device_id={"mp": z - 1}, device_id_type=MESH)

    @pl.when(z < n - 1)
    def _():
        pl.semaphore_signal(barrier, inc=1, device_id={"mp": z + 1}, device_id_type=MESH)

    line_peers = jnp.where(z > 0, 1, 0) + jnp.where(z < n - 1, 1, 0)
    pl.semaphore_wait(barrier, n_dp + line_peers)

    def rows_of(c):
        return pl.ds(c * part_rows, part_rows)

    def send_block(src, slot, c, send_sem, device_id):
        return pltpu.make_async_remote_copy(
            src_ref=src,
            dst_ref=mem_all.at[slot, rows_of(c)],
            send_sem=send_sem,
            recv_sem=ag_recv.at[slot, c],
            device_id=device_id,
            device_id_type=MESH,
        )

    def own_to_left(c):
        return send_block(mem_all.at[own_slot, rows_of(c)], own_slot, c, ag_own_send.at[0, c], {"mp": z - 1})

    def own_to_right(c):
        return send_block(mem_all.at[own_slot, rows_of(c)], own_slot, c, ag_own_send.at[1, c], {"mp": z + 1})

    def to_x(k, c):
        slot = x * n + near[k]
        return send_block(mem_all.at[slot, rows_of(c)], slot, c, ag_x_send.at[k, c], {"section": other})

    def relay(k, c):
        slot = x * n + near[k]
        dest = jnp.where(near[k] < z, z + 1, z - 1)
        return send_block(mem_all.at[slot, rows_of(c)], slot, c, ag_z_send.at[k, c], {"mp": dest})

    def relays(k):
        j = near[k]
        return ((j < z) & (z < n - 1)) | ((j > z) & (z > 0))

    def arrived(slot, c):
        send_block(mem_all.at[slot, rows_of(c)], slot, c, ag_x_send.at[0, c], {"section": other}).wait_recv()

    loads[0].wait()
    for c in range(CHUNKS):

        @pl.when(z > 0)
        def _():
            own_to_left(c).start()

        @pl.when(z < n - 1)
        def _():
            own_to_right(c).start()

        to_x(0, c).start()

    def send_length(r):
        peer = lax.rem(dp + r, n_dp)
        return pltpu.make_async_remote_copy(
            src_ref=len_own,
            dst_ref=len_all.at[dp],
            send_sem=len_send.at[r],
            recv_sem=len_recv.at[dp],
            device_id={"dp": peer},
            device_id_type=MESH,
        )

    for r in range(1, n_dp):
        send_length(r).start()

    loads[1].wait()
    q_t[...] = q[...].T
    k_acc[...] = jnp.zeros_like(k_acc)
    v_acc[...] = jnp.zeros_like(v_acc)
    loads[2].wait()

    valid = (
        lax.broadcasted_iota(jnp.int32, (seq_rows, 1), 0) < length
    ).astype(jnp.float32)
    for k in range(1, n):
        for c in range(CHUNKS):
            arrived(x * n + near[k], c)

            @pl.when(relays(k))
            def _():
                relay(k, c).start()

            to_x(k, c).start()
        if k == 1:
            total = len_own[...]
            for r in range(1, n_dp):
                peer = lax.rem(dp + r, n_dp)
                pltpu.make_async_remote_copy(
                    src_ref=len_own,
                    dst_ref=len_all.at[peer],
                    send_sem=len_send.at[r],
                    recv_sem=len_recv.at[peer],
                    device_id={"dp": peer},
                    device_id_type=MESH,
                ).wait_recv()
                total = total + len_all[peer]
            loss_weight = (float(n_dp * seq_rows) / total)[0:1, 0:1]
            weighted = (cot[...].astype(jnp.float32) * (valid * loss_weight)).astype(jnp.bfloat16)
            w[...] = weighted
            w_t[...] = weighted.T
    loads[3].wait()
    loads[4].wait()

    @pl.loop(0, 2 * n)
    def _(e):
        own_row = e < n
        slot = jnp.where(own_row, x * n, other * n) + pick(near, jnp.where(own_row, e, e - n))

        @pl.when(e >= n)
        def _():
            for c in range(CHUNKS):
                arrived(slot, c)

        rows = pl.ds(pl.multiple_of(slot * block, block), block)
        mem_block = mem_all[slot]
        k_acc[...] += jnp.dot(mem_block, kw[rows, :], preferred_element_type=jnp.float32)
        v_acc[...] += jnp.dot(mem_block, vw[rows, :], preferred_element_type=jnp.float32)

    last = (((1,), (1,)), ((), ()))

    @pl.loop(0, heads)
    def _(h):
        cols = pl.ds(pl.multiple_of(h * HEAD_DIM, HEAD_DIM), HEAD_DIM)
        key_h = k_acc[:, cols].astype(jnp.bfloat16)
        value_h = v_acc[:, cols].astype(jnp.bfloat16)
        scores = (
            lax.dot_general(q[:, cols], key_h, last, preferred_element_type=jnp.float32)
            * score_scale
        )
        prob_grad = lax.dot_general(w[:, cols], value_h, last, preferred_element_type=jnp.float32)
        top = jnp.max(scores, axis=-1, keepdims=True)
        powers = jnp.exp(scores - top)
        attention = powers / jnp.sum(powers, axis=-1, keepdims=True)
        attention_low = attention.astype(jnp.bfloat16)
        row_dot = jnp.sum(attention * prob_grad, axis=-1, keepdims=True)
        score_grad = (attention * (prob_grad - row_dot) * score_scale).astype(jnp.bfloat16)
        dv_t[cols, :] = jnp.dot(
            w_t[cols, :], attention_low, preferred_element_type=jnp.float32
        ).astype(jnp.bfloat16)
        dk_t[cols, :] = jnp.dot(
            q_t[cols, :], score_grad, preferred_element_type=jnp.float32
        ).astype(jnp.bfloat16)
        context = jnp.dot(attention_low, value_h, preferred_element_type=jnp.float32)
        ctx[:, cols] = (context * valid).astype(jnp.bfloat16)
    ctx_copy = pltpu.make_async_copy(ctx, ctx_out, local_sem.at[0])
    ctx_copy.start()

    def feats_of(c):
        return pl.ds(c * part_feats, part_feats)

    def sum_to_x(j, c):
        return pltpu.make_async_remote_copy(
            src_ref=xs.at[j, feats_of(c)],
            dst_ref=xr.at[j, feats_of(c)],
            send_sem=rs_x_send.at[j, c],
            recv_sem=rs_x_recv.at[j, c],
            device_id={"section": other},
            device_id_type=MESH,
        )

    def sum_along_z(j, c, slot):
        dest = jnp.where(j > z, z + 1, z - 1)
        return pltpu.make_async_remote_copy(
            src_ref=zs.at[j, feats_of(c)],
            dst_ref=zr.at[slot, feats_of(c)],
            send_sem=rs_z_send.at[j, c],
            recv_sem=rs_z_recv.at[slot, c],
            device_id={"mp": dest},
            device_id_type=MESH,
        )

    @pl.loop(0, 2 * n)
    def _(e):
        sent = e < n
        j = pick(far, jnp.where(sent, e, e - n))
        slot = jnp.where(sent, other * n, x * n) + j
        rows = pl.ds(pl.multiple_of(slot * block, block), block)
        acc[j] = jnp.dot(
            kw[rows, :], dk_t[...], preferred_element_type=jnp.float32
        ) + jnp.dot(vw[rows, :], dv_t[...], preferred_element_type=jnp.float32)

        @pl.when(sent)
        def _():
            xs[j] = acc[j].astype(jnp.bfloat16)
            for c in range(CHUNKS):
                sum_to_x(j, c).start()

    def target_slot(j):
        return jnp.where((j < z) & (z - 1 == j), n, j)

    @pl.loop(0, n - 1)
    def _(k):
        j = pick(far, k)
        has_source = ((j > z) & (z > 0)) | ((j < z) & (z < n - 1))
        for c in range(CHUNKS):
            sum_to_x(j, c).wait_recv()
            acc[j, feats_of(c)] += xr[j, feats_of(c)].astype(jnp.float32)

            @pl.when(has_source)
            def _():
                sum_along_z(j, c, j).wait_recv()
                acc[j, feats_of(c)] += zr[j, feats_of(c)].astype(jnp.float32)

            zs[j, feats_of(c)] = acc[j, feats_of(c)].astype(jnp.bfloat16)
            sum_along_z(j, c, target_slot(j)).start()

    for c in range(CHUNKS):
        sum_to_x(z, c).wait_recv()
        grad_out[feats_of(c)] = acc[z, feats_of(c)] + xr[z, feats_of(c)].astype(jnp.float32)

        @pl.when(z > 0)
        def _():
            sum_along_z(far[0], c, z).wait_recv()
            grad_out[feats_of(c)] += zr[z, feats_of(c)].astype(jnp.float32)

        @pl.when(z < n - 1)
        def _():
            sum_along_z(far[0], c, n).wait_recv()
            grad_out[feats_of(c)] += zr[n, feats_of(c)].astype(jnp.float32)

    for c in range(CHUNKS):

        @pl.when(z > 0)
        def _():
            own_to_left(c).wait_send()

        @pl.when(z < n - 1)
        def _():
            own_to_right(c).wait_send()

        for k in range(n):
            to_x(k, c).wait_send()
            sum_to_x(far[k], c).wait_send()
        for k in range(1, n):

            @pl.when(relays(k))
            def _():
                relay(k, c).wait_send()

        for k in range(n - 1):
            sum_along_z(far[k], c, target_slot(far[k])).wait_send()
    for r in range(1, n_dp):
        send_length(r).wait_send()
    ctx_copy.wait()


def fused(n, n_dp, memory, key_weight, value_weight, queries, cotangent, target_lengths):
    mem_rows, block = memory.shape[1:]
    feats, width = key_weight.shape[1:]
    seq_rows = queries.shape[2]
    low, full = jnp.bfloat16, jnp.float32
    vmem, sem = pltpu.VMEM, pltpu.SemaphoreType.DMA
    anywhere = pl.BlockSpec(memory_space=pl.ANY)
    context, grad = pl.pallas_call(
        functools.partial(fused_kernel, n, n_dp),
        out_shape=(
            jax.ShapeDtypeStruct((seq_rows, width), low),
            jax.ShapeDtypeStruct((block, mem_rows), full),
        ),
        in_specs=[pl.BlockSpec(memory_space=pltpu.SMEM)] + [anywhere] * 5,
        out_specs=(anywhere, pl.BlockSpec(memory_space=pltpu.VMEM)),
        scratch_shapes=[
            vmem((feats, width), low),
            vmem((feats, width), low),
            vmem((seq_rows, width), low),
            vmem((seq_rows, width), low),
            vmem((2 * n, mem_rows, block), low),
            vmem((mem_rows, width), full),
            vmem((mem_rows, width), full),
            vmem((width, seq_rows), low),
            vmem((seq_rows, width), low),
            vmem((width, seq_rows), low),
            vmem((seq_rows, width), low),
            vmem((width, mem_rows), low),
            vmem((width, mem_rows), low),
            vmem((n, block, mem_rows), low),
            vmem((n, block, mem_rows), low),
            vmem((n, block, mem_rows), full),
            vmem((n, block, mem_rows), low),
            vmem((n + 1, block, mem_rows), low),
            vmem((8, 128), full),
            vmem((n_dp, 8, 128), full),
            sem((5,)),
            sem((2, CHUNKS)),
            sem((n, CHUNKS)),
            sem((n, CHUNKS)),
            sem((2 * n, CHUNKS)),
            sem((n, CHUNKS)),
            sem((n, CHUNKS)),
            sem((n, CHUNKS)),
            sem((n + 1, CHUNKS)),
            sem((n_dp,)),
            sem((n_dp,)),
        ],
        compiler_params=pltpu.CompilerParams(
            collective_id=0, has_side_effects=True, vmem_limit_bytes=60 * 1024 * 1024
        ),
    )(
        target_lengths,
        memory[0],
        key_weight[0],
        value_weight[0],
        queries[0, 0],
        cotangent[0, 0],
    )
    context, grad = pl.pallas_call(
        finish_kernel,
        out_shape=(
            jax.ShapeDtypeStruct((seq_rows, width), low),
            jax.ShapeDtypeStruct((mem_rows, block), full),
        ),
        in_specs=[anywhere] * 2,
        out_specs=(anywhere, anywhere),
        scratch_shapes=[
            vmem((seq_rows, width), low),
            vmem((block, mem_rows), full),
            vmem((mem_rows, block), full),
            sem((4,)),
        ],
        compiler_params=pltpu.CompilerParams(vmem_limit_bytes=60 * 1024 * 1024),
    )(context, grad)
    return context[None, None], grad[None]


def on_device(memory, key_weight, value_weight, queries, cotangent, target_lengths):
    width = key_weight.shape[2]
    head_count = width // HEAD_DIM
    seq_rows = queries.shape[2]
    score_scale = HEAD_DIM ** (-0.5)
    mem_block = memory[0]
    mem_rows = mem_block.shape[0]
    full_memory = lax.all_gather(mem_block, ("section", "mp"), axis=1, tiled=True)
    token_total = lax.psum(target_lengths.astype(jnp.float32), "dp")
    slot_total = float(lax.axis_size("dp") * target_lengths.shape[0] * seq_rows)
    loss_weight = slot_total / token_total[0]
    valid = (jnp.arange(seq_rows, dtype=jnp.int32) < target_lengths[0]).astype(jnp.float32)
    layer_index = 0
    key_rows = jnp.dot(
        full_memory, key_weight[layer_index], preferred_element_type=jnp.float32
    ).astype(jnp.bfloat16)
    value_rows = jnp.dot(
        full_memory, value_weight[layer_index], preferred_element_type=jnp.float32
    ).astype(jnp.bfloat16)
    key_heads = key_rows.reshape(mem_rows, head_count, HEAD_DIM)
    value_heads = value_rows.reshape(mem_rows, head_count, HEAD_DIM)
    query_heads = queries[layer_index, 0].reshape(seq_rows, head_count, HEAD_DIM)
    scores = (
        jnp.einsum("thd,shd->hts", query_heads, key_heads, preferred_element_type=jnp.float32)
        * score_scale
    )
    attention = jax.nn.softmax(scores, axis=-1)
    attention_low = attention.astype(jnp.bfloat16)
    context = jnp.einsum(
        "hts,shd->thd", attention_low, value_heads, preferred_element_type=jnp.float32
    )
    context = (context * valid[:, None, None]).astype(jnp.bfloat16)
    contexts = [context.reshape(seq_rows, width)]
    weighted = cotangent[layer_index, 0].astype(jnp.float32) * (valid * loss_weight)[:, None]
    weighted = weighted.astype(jnp.bfloat16).reshape(seq_rows, head_count, HEAD_DIM)
    value_grad = jnp.einsum(
        "hts,thd->shd", attention_low, weighted, preferred_element_type=jnp.float32
    )
    value_grads = [value_grad.astype(jnp.bfloat16).reshape(mem_rows, width)]
    prob_grad = jnp.einsum(
        "thd,shd->hts", weighted, value_heads, preferred_element_type=jnp.float32
    )
    row_dot = jnp.sum(attention * prob_grad, axis=-1, keepdims=True)
    score_grad = (attention * (prob_grad - row_dot) * score_scale).astype(jnp.bfloat16)
    key_grad = jnp.einsum(
        "hts,thd->shd", score_grad, query_heads, preferred_element_type=jnp.float32
    )
    key_grads = [key_grad.astype(jnp.bfloat16).reshape(mem_rows, width)]
    contract_last = (((1,), (1,)), ((), ()))
    layer_index = 0
    key_part = key_weight[layer_index]
    value_part = value_weight[layer_index]
    running = lax.dot_general(
        key_part, key_grads[layer_index], contract_last, preferred_element_type=jnp.float32
    )
    running = running + lax.dot_general(
        value_part, value_grads[layer_index], contract_last, preferred_element_type=jnp.float32
    )
    section_part = lax.psum_scatter(
        running.astype(jnp.bfloat16), "section", scatter_dimension=0, tiled=True
    )
    own_part = lax.psum_scatter(section_part, "mp", scatter_dimension=0, tiled=True).astype(
        jnp.float32
    )
    own_grad = own_part.T
    context_out = jnp.stack(contexts, axis=0)[:, None]
    return (context_out, own_grad[None])


def solution(mesh):
    sections, n, n_dp = mesh.shape["section"], mesh.shape["mp"], mesh.shape["dp"]

    def per_device(memory, key_weight, value_weight, queries, cotangent, target_lengths):
        args = (memory, key_weight, value_weight, queries, cotangent, target_lengths)
        mem_rows, block = memory.shape[1:]
        if sections == 2 and n >= 2 and mem_rows % 128 == 0 and block % 128 == 0:
            return fused(n, n_dp, *args)
        return on_device(*args)

    return jax.shard_map(
        per_device,
        mesh=mesh,
        in_specs=(
            P("dp", None, ("section", "mp")),
            P("section", None, "mp"),
            P("section", None, "mp"),
            P("section", "dp", None, "mp"),
            P("section", "dp", None, "mp"),
            P("dp"),
        ),
        out_specs=(P("section", "dp", None, "mp"), P("dp", None, ("section", "mp"))),
        check_vma=False,
    )
```

```python
import functools

import jax
import jax.numpy as jnp
from jax import lax
from jax.experimental import pallas as pl
from jax.experimental.pallas import tpu as pltpu
from jax.sharding import PartitionSpec as P

HEAD_DIM = 256
CHUNKS = 2
MESH = pl.DeviceIdType.MESH


def far_to_near(z, n):
    low, high, order = 0, n - 1, []
    for _ in range(n):
        take_low = (z - low) >= (high - z)
        order.append(jnp.where(take_low, low, high))
        low, high = jnp.where(take_low, low + 1, low), jnp.where(take_low, high, high - 1)
    return order


def pick(order, at):
    found = order[0]
    for i in range(1, len(order)):
        found = jnp.where(at == i, order[i], found)
    return found


def finish_kernel(ctx_ref, grad_ref, ctx_out, grad_out, ctx, grad, grad_t, sems):
    grad_load = pltpu.make_async_copy(grad_ref, grad, sems.at[0])
    ctx_load = pltpu.make_async_copy(ctx_ref, ctx, sems.at[1])
    grad_load.start()
    ctx_load.start()
    grad_load.wait()
    grad_t[...] = grad[...].T
    grad_store = pltpu.make_async_copy(grad_t, grad_out, sems.at[2])
    grad_store.start()
    ctx_load.wait()
    ctx_store = pltpu.make_async_copy(ctx, ctx_out, sems.at[3])
    ctx_store.start()
    grad_store.wait()
    ctx_store.wait()


def fused_kernel(
    n, n_dp,
    len_ref, memory_ref, kw_ref, vw_ref, q_ref, cot_ref,
    ctx_out, grad_out,
    kw, vw, q, cot, mem_all, k_acc, v_acc, q_t, w, w_t, ctx, dk_t, dv_t,
    xs, xr, acc, zs, zr, len_own, len_all,
    local_sem, ag_z_send, ag_x_send, ag_recv,
    rs_x_send, rs_x_recv, rs_z_send, rs_z_recv, len_send, len_recv,
):
    x = lax.axis_index("section")
    z = lax.axis_index("mp")
    dp = lax.axis_index("dp")
    other = 1 - x
    mem_rows, block = memory_ref.shape
    seq_rows, width = q_ref.shape
    heads = width // HEAD_DIM
    score_scale = HEAD_DIM ** (-0.5)
    part_rows = mem_rows // CHUNKS
    part_feats = block // CHUNKS
    far = far_to_near(z, n)
    near = far[::-1]

    own_slot = x * n + z
    loads = [
        pltpu.make_async_copy(src, dst, local_sem.at[i])
        for i, (src, dst) in enumerate(
            (
                (memory_ref, mem_all.at[own_slot]),
                (q_ref, q),
                (cot_ref, cot),
                (kw_ref, kw),
                (vw_ref, vw),
            )
        )
    ]
    for load in loads:
        load.start()
    length = len_ref[0]
    len_own[...] = jnp.full(len_own.shape, length.astype(jnp.float32), jnp.float32)

    barrier = pltpu.get_barrier_semaphore()
    pl.semaphore_signal(barrier, inc=1, device_id={"section": other}, device_id_type=MESH)
    for r in range(1, n_dp):
        peer = lax.rem(dp + r, n_dp)
        pl.semaphore_signal(barrier, inc=1, device_id={"dp": peer}, device_id_type=MESH)

    for k in range(1, n):
        pl.semaphore_signal(barrier, inc=1, device_id={"mp": near[k]}, device_id_type=MESH)
    pl.semaphore_wait(barrier, n_dp + n - 1)

    def rows_of(c):
        return pl.ds(c * part_rows, part_rows)

    def send_block(src, slot, c, send_sem, device_id):
        return pltpu.make_async_remote_copy(
            src_ref=src,
            dst_ref=mem_all.at[slot, rows_of(c)],
            send_sem=send_sem,
            recv_sem=ag_recv.at[slot, c],
            device_id=device_id,
            device_id_type=MESH,
        )

    def to_line(k, c):
        return send_block(
            mem_all.at[own_slot, rows_of(c)], own_slot, c, ag_z_send.at[k, c], {"mp": near[k]}
        )

    def to_x(k, c):
        slot = x * n + near[k]
        return send_block(mem_all.at[slot, rows_of(c)], slot, c, ag_x_send.at[k, c], {"section": other})

    def arrived(slot, c):
        send_block(mem_all.at[slot, rows_of(c)], slot, c, ag_x_send.at[0, c], {"section": other}).wait_recv()

    loads[0].wait()
    for c in range(CHUNKS):
        to_line(1, c).start()
        to_x(0, c).start()
    for k in range(2, n):
        for c in range(CHUNKS):
            to_line(k, c).start()

    def send_length(r):
        peer = lax.rem(dp + r, n_dp)
        return pltpu.make_async_remote_copy(
            src_ref=len_own,
            dst_ref=len_all.at[dp],
            send_sem=len_send.at[r],
            recv_sem=len_recv.at[dp],
            device_id={"dp": peer},
            device_id_type=MESH,
        )

    for r in range(1, n_dp):
        send_length(r).start()

    loads[1].wait()
    q_t[...] = q[...].T
    k_acc[...] = jnp.zeros_like(k_acc)
    v_acc[...] = jnp.zeros_like(v_acc)
    loads[2].wait()

    valid = (
        lax.broadcasted_iota(jnp.int32, (seq_rows, 1), 0) < length
    ).astype(jnp.float32)
    for k in range(1, n):
        for c in range(CHUNKS):
            arrived(x * n + near[k], c)
            to_x(k, c).start()
        if k == 1:
            total = len_own[...]
            for r in range(1, n_dp):
                peer = lax.rem(dp + r, n_dp)
                pltpu.make_async_remote_copy(
                    src_ref=len_own,
                    dst_ref=len_all.at[peer],
                    send_sem=len_send.at[r],
                    recv_sem=len_recv.at[peer],
                    device_id={"dp": peer},
                    device_id_type=MESH,
                ).wait_recv()
                total = total + len_all[peer]
            loss_weight = (float(n_dp * seq_rows) / total)[0:1, 0:1]
            weighted = (cot[...].astype(jnp.float32) * (valid * loss_weight)).astype(jnp.bfloat16)
            w[...] = weighted
            w_t[...] = weighted.T
    loads[3].wait()
    loads[4].wait()

    @pl.loop(0, 2 * n)
    def _(e):
        own_row = e < n
        slot = jnp.where(own_row, x * n, other * n) + pick(near, jnp.where(own_row, e, e - n))

        @pl.when(e >= n)
        def _():
            for c in range(CHUNKS):
                arrived(slot, c)

        rows = pl.ds(pl.multiple_of(slot * block, block), block)
        mem_block = mem_all[slot]
        k_acc[...] += jnp.dot(mem_block, kw[rows, :], preferred_element_type=jnp.float32)
        v_acc[...] += jnp.dot(mem_block, vw[rows, :], preferred_element_type=jnp.float32)

    last = (((1,), (1,)), ((), ()))

    @pl.loop(0, heads)
    def _(h):
        cols = pl.ds(pl.multiple_of(h * HEAD_DIM, HEAD_DIM), HEAD_DIM)
        key_h = k_acc[:, cols].astype(jnp.bfloat16)
        value_h = v_acc[:, cols].astype(jnp.bfloat16)
        scores = (
            lax.dot_general(q[:, cols], key_h, last, preferred_element_type=jnp.float32)
            * score_scale
        )
        prob_grad = lax.dot_general(w[:, cols], value_h, last, preferred_element_type=jnp.float32)
        top = jnp.max(scores, axis=-1, keepdims=True)
        powers = jnp.exp(scores - top)
        attention = powers / jnp.sum(powers, axis=-1, keepdims=True)
        attention_low = attention.astype(jnp.bfloat16)
        row_dot = jnp.sum(attention * prob_grad, axis=-1, keepdims=True)
        score_grad = (attention * (prob_grad - row_dot) * score_scale).astype(jnp.bfloat16)
        dv_t[cols, :] = jnp.dot(
            w_t[cols, :], attention_low, preferred_element_type=jnp.float32
        ).astype(jnp.bfloat16)
        dk_t[cols, :] = jnp.dot(
            q_t[cols, :], score_grad, preferred_element_type=jnp.float32
        ).astype(jnp.bfloat16)
        context = jnp.dot(attention_low, value_h, preferred_element_type=jnp.float32)
        ctx[:, cols] = (context * valid).astype(jnp.bfloat16)
    ctx_copy = pltpu.make_async_copy(ctx, ctx_out, local_sem.at[0])
    ctx_copy.start()

    def feats_of(c):
        return pl.ds(c * part_feats, part_feats)

    def sum_to_x(j, c):
        return pltpu.make_async_remote_copy(
            src_ref=xs.at[j, feats_of(c)],
            dst_ref=xr.at[j, feats_of(c)],
            send_sem=rs_x_send.at[j, c],
            recv_sem=rs_x_recv.at[j, c],
            device_id={"section": other},
            device_id_type=MESH,
        )

    def sum_along_z(j, c, slot):
        return pltpu.make_async_remote_copy(
            src_ref=zs.at[j, feats_of(c)],
            dst_ref=zr.at[slot, feats_of(c)],
            send_sem=rs_z_send.at[j, c],
            recv_sem=rs_z_recv.at[slot, c],
            device_id={"mp": j},
            device_id_type=MESH,
        )

    @pl.loop(0, 2 * n)
    def _(e):
        sent = e < n
        j = pick(far, jnp.where(sent, e, e - n))
        slot = jnp.where(sent, other * n, x * n) + j
        rows = pl.ds(pl.multiple_of(slot * block, block), block)
        acc[j] = jnp.dot(
            kw[rows, :], dk_t[...], preferred_element_type=jnp.float32
        ) + jnp.dot(vw[rows, :], dv_t[...], preferred_element_type=jnp.float32)

        @pl.when(sent)
        def _():
            xs[j] = acc[j].astype(jnp.bfloat16)
            for c in range(CHUNKS):
                sum_to_x(j, c).start()

    @pl.loop(0, n - 1)
    def _(k):
        j = pick(far, k)
        for c in range(CHUNKS):
            sum_to_x(j, c).wait_recv()
            zs[j, feats_of(c)] = (
                acc[j, feats_of(c)] + xr[j, feats_of(c)].astype(jnp.float32)
            ).astype(jnp.bfloat16)
            sum_along_z(j, c, z).start()

    for c in range(CHUNKS):
        sum_to_x(z, c).wait_recv()
        total = acc[z, feats_of(c)] + xr[z, feats_of(c)].astype(jnp.float32)
        for k in range(1, n):
            sum_along_z(near[k], c, near[k]).wait_recv()
            total = total + zr[near[k], feats_of(c)].astype(jnp.float32)
        grad_out[feats_of(c)] = total

    for c in range(CHUNKS):
        for k in range(n):
            to_x(k, c).wait_send()
            sum_to_x(far[k], c).wait_send()
        for k in range(1, n):
            to_line(k, c).wait_send()
            sum_along_z(near[k], c, z).wait_send()
    for r in range(1, n_dp):
        send_length(r).wait_send()
    ctx_copy.wait()


def fused(n, n_dp, memory, key_weight, value_weight, queries, cotangent, target_lengths):
    mem_rows, block = memory.shape[1:]
    feats, width = key_weight.shape[1:]
    seq_rows = queries.shape[2]
    low, full = jnp.bfloat16, jnp.float32
    vmem, sem = pltpu.VMEM, pltpu.SemaphoreType.DMA
    anywhere = pl.BlockSpec(memory_space=pl.ANY)
    context, grad = pl.pallas_call(
        functools.partial(fused_kernel, n, n_dp),
        out_shape=(
            jax.ShapeDtypeStruct((seq_rows, width), low),
            jax.ShapeDtypeStruct((block, mem_rows), full),
        ),
        in_specs=[pl.BlockSpec(memory_space=pltpu.SMEM)] + [anywhere] * 5,
        out_specs=(anywhere, pl.BlockSpec(memory_space=pltpu.VMEM)),
        scratch_shapes=[
            vmem((feats, width), low),
            vmem((feats, width), low),
            vmem((seq_rows, width), low),
            vmem((seq_rows, width), low),
            vmem((2 * n, mem_rows, block), low),
            vmem((mem_rows, width), full),
            vmem((mem_rows, width), full),
            vmem((width, seq_rows), low),
            vmem((seq_rows, width), low),
            vmem((width, seq_rows), low),
            vmem((seq_rows, width), low),
            vmem((width, mem_rows), low),
            vmem((width, mem_rows), low),
            vmem((n, block, mem_rows), low),
            vmem((n, block, mem_rows), low),
            vmem((n, block, mem_rows), full),
            vmem((n, block, mem_rows), low),
            vmem((n, block, mem_rows), low),
            vmem((8, 128), full),
            vmem((n_dp, 8, 128), full),
            sem((5,)),
            sem((n, CHUNKS)),
            sem((n, CHUNKS)),
            sem((2 * n, CHUNKS)),
            sem((n, CHUNKS)),
            sem((n, CHUNKS)),
            sem((n, CHUNKS)),
            sem((n, CHUNKS)),
            sem((n_dp,)),
            sem((n_dp,)),
        ],
        compiler_params=pltpu.CompilerParams(
            collective_id=0, has_side_effects=True, vmem_limit_bytes=60 * 1024 * 1024
        ),
    )(
        target_lengths,
        memory[0],
        key_weight[0],
        value_weight[0],
        queries[0, 0],
        cotangent[0, 0],
    )
    context, grad = pl.pallas_call(
        finish_kernel,
        out_shape=(
            jax.ShapeDtypeStruct((seq_rows, width), low),
            jax.ShapeDtypeStruct((mem_rows, block), full),
        ),
        in_specs=[anywhere] * 2,
        out_specs=(anywhere, anywhere),
        scratch_shapes=[
            vmem((seq_rows, width), low),
            vmem((block, mem_rows), full),
            vmem((mem_rows, block), full),
            sem((4,)),
        ],
        compiler_params=pltpu.CompilerParams(vmem_limit_bytes=60 * 1024 * 1024),
    )(context, grad)
    return context[None, None], grad[None]


def on_device(memory, key_weight, value_weight, queries, cotangent, target_lengths):
    width = key_weight.shape[2]
    head_count = width // HEAD_DIM
    seq_rows = queries.shape[2]
    score_scale = HEAD_DIM ** (-0.5)
    mem_block = memory[0]
    mem_rows = mem_block.shape[0]
    full_memory = lax.all_gather(mem_block, ("section", "mp"), axis=1, tiled=True)
    token_total = lax.psum(target_lengths.astype(jnp.float32), "dp")
    slot_total = float(lax.axis_size("dp") * target_lengths.shape[0] * seq_rows)
    loss_weight = slot_total / token_total[0]
    valid = (jnp.arange(seq_rows, dtype=jnp.int32) < target_lengths[0]).astype(jnp.float32)
    layer_index = 0
    key_rows = jnp.dot(
        full_memory, key_weight[layer_index], preferred_element_type=jnp.float32
    ).astype(jnp.bfloat16)
    value_rows = jnp.dot(
        full_memory, value_weight[layer_index], preferred_element_type=jnp.float32
    ).astype(jnp.bfloat16)
    key_heads = key_rows.reshape(mem_rows, head_count, HEAD_DIM)
    value_heads = value_rows.reshape(mem_rows, head_count, HEAD_DIM)
    query_heads = queries[layer_index, 0].reshape(seq_rows, head_count, HEAD_DIM)
    scores = (
        jnp.einsum("thd,shd->hts", query_heads, key_heads, preferred_element_type=jnp.float32)
        * score_scale
    )
    attention = jax.nn.softmax(scores, axis=-1)
    attention_low = attention.astype(jnp.bfloat16)
    context = jnp.einsum(
        "hts,shd->thd", attention_low, value_heads, preferred_element_type=jnp.float32
    )
    context = (context * valid[:, None, None]).astype(jnp.bfloat16)
    contexts = [context.reshape(seq_rows, width)]
    weighted = cotangent[layer_index, 0].astype(jnp.float32) * (valid * loss_weight)[:, None]
    weighted = weighted.astype(jnp.bfloat16).reshape(seq_rows, head_count, HEAD_DIM)
    value_grad = jnp.einsum(
        "hts,thd->shd", attention_low, weighted, preferred_element_type=jnp.float32
    )
    value_grads = [value_grad.astype(jnp.bfloat16).reshape(mem_rows, width)]
    prob_grad = jnp.einsum(
        "thd,shd->hts", weighted, value_heads, preferred_element_type=jnp.float32
    )
    row_dot = jnp.sum(attention * prob_grad, axis=-1, keepdims=True)
    score_grad = (attention * (prob_grad - row_dot) * score_scale).astype(jnp.bfloat16)
    key_grad = jnp.einsum(
        "hts,thd->shd", score_grad, query_heads, preferred_element_type=jnp.float32
    )
    key_grads = [key_grad.astype(jnp.bfloat16).reshape(mem_rows, width)]
    contract_last = (((1,), (1,)), ((), ()))
    layer_index = 0
    key_part = key_weight[layer_index]
    value_part = value_weight[layer_index]
    running = lax.dot_general(
        key_part, key_grads[layer_index], contract_last, preferred_element_type=jnp.float32
    )
    running = running + lax.dot_general(
        value_part, value_grads[layer_index], contract_last, preferred_element_type=jnp.float32
    )
    section_part = lax.psum_scatter(
        running.astype(jnp.bfloat16), "section", scatter_dimension=0, tiled=True
    )
    own_part = lax.psum_scatter(section_part, "mp", scatter_dimension=0, tiled=True).astype(
        jnp.float32
    )
    own_grad = own_part.T
    context_out = jnp.stack(contexts, axis=0)[:, None]
    return (context_out, own_grad[None])


def solution(mesh):
    sections, n, n_dp = mesh.shape["section"], mesh.shape["mp"], mesh.shape["dp"]

    def per_device(memory, key_weight, value_weight, queries, cotangent, target_lengths):
        args = (memory, key_weight, value_weight, queries, cotangent, target_lengths)
        mem_rows, block = memory.shape[1:]
        if sections == 2 and n >= 2 and mem_rows % 128 == 0 and block % 128 == 0:
            return fused(n, n_dp, *args)
        return on_device(*args)

    return jax.shard_map(
        per_device,
        mesh=mesh,
        in_specs=(
            P("dp", None, ("section", "mp")),
            P("section", None, "mp"),
            P("section", None, "mp"),
            P("section", "dp", None, "mp"),
            P("section", "dp", None, "mp"),
            P("dp"),
        ),
        out_specs=(P("section", "dp", None, "mp"), P("dp", None, ("section", "mp"))),
        check_vma=False,
    )
```

```python
import functools

import jax
import jax.numpy as jnp
from jax import lax
from jax.experimental import pallas as pl
from jax.experimental.pallas import tpu as pltpu
from jax.sharding import PartitionSpec as P

HEAD_DIM = 256
CHUNKS = 2
TURN_AT = 2
MESH = pl.DeviceIdType.MESH


def far_to_near(z, n):
    low, high, order = 0, n - 1, []
    for _ in range(n):
        take_low = (z - low) >= (high - z)
        order.append(jnp.where(take_low, low, high))
        low, high = jnp.where(take_low, low + 1, low), jnp.where(take_low, high, high - 1)
    return order


def pick(order, at):
    found = order[0]
    for i in range(1, len(order)):
        found = jnp.where(at == i, order[i], found)
    return found


def finish_kernel(ctx_ref, grad_ref, ctx_out, grad_out, ctx, grad, grad_t, sems):
    grad_load = pltpu.make_async_copy(grad_ref, grad, sems.at[0])
    ctx_load = pltpu.make_async_copy(ctx_ref, ctx, sems.at[1])
    grad_load.start()
    ctx_load.start()
    grad_load.wait()
    grad_t[...] = grad[...].T
    grad_store = pltpu.make_async_copy(grad_t, grad_out, sems.at[2])
    grad_store.start()
    ctx_load.wait()
    ctx_store = pltpu.make_async_copy(ctx, ctx_out, sems.at[3])
    ctx_store.start()
    grad_store.wait()
    ctx_store.wait()


def fused_kernel(
    n, n_dp,
    len_ref, memory_ref, kw_ref, vw_ref, q_ref, cot_ref,
    ctx_out, grad_out,
    kw, vw, q, cot, mem_all, k_acc, v_acc, q_t, w, w_t, ctx, dk_t, dv_t,
    xs, xr, acc, zs, zr, len_own, len_all,
    local_sem, ag_own_send, ag_z_send, ag_x_send, ag_recv,
    rs_x_send, rs_x_recv, rs_z_send, rs_z_recv, len_send, len_recv, turn_sem,
):
    x = lax.axis_index("section")
    z = lax.axis_index("mp")
    dp = lax.axis_index("dp")
    other = 1 - x
    mem_rows, block = memory_ref.shape
    seq_rows, width = q_ref.shape
    heads = width // HEAD_DIM
    score_scale = HEAD_DIM ** (-0.5)
    part_rows = mem_rows // CHUNKS
    part_feats = block // CHUNKS
    far = far_to_near(z, n)
    near = far[::-1]

    own_slot = x * n + z
    loads = [
        pltpu.make_async_copy(src, dst, local_sem.at[i])
        for i, (src, dst) in enumerate(
            (
                (memory_ref, mem_all.at[own_slot]),
                (q_ref, q),
                (cot_ref, cot),
                (kw_ref, kw),
                (vw_ref, vw),
            )
        )
    ]
    for load in loads:
        load.start()
    length = len_ref[0]
    len_own[...] = jnp.full(len_own.shape, length.astype(jnp.float32), jnp.float32)

    barrier = pltpu.get_barrier_semaphore()
    pl.semaphore_signal(barrier, inc=1, device_id={"section": other}, device_id_type=MESH)
    for r in range(1, n_dp):
        peer = lax.rem(dp + r, n_dp)
        pl.semaphore_signal(barrier, inc=1, device_id={"dp": peer}, device_id_type=MESH)

    @pl.when(z > 0)
    def _():
        pl.semaphore_signal(barrier, inc=1, device_id={"mp": z - 1}, device_id_type=MESH)

    @pl.when(z < n - 1)
    def _():
        pl.semaphore_signal(barrier, inc=1, device_id={"mp": z + 1}, device_id_type=MESH)

    line_peers = jnp.where(z > 0, 1, 0) + jnp.where(z < n - 1, 1, 0)
    pl.semaphore_wait(barrier, n_dp + line_peers)

    def rows_of(c):
        return pl.ds(c * part_rows, part_rows)

    def send_block(src, slot, c, send_sem, device_id):
        return pltpu.make_async_remote_copy(
            src_ref=src,
            dst_ref=mem_all.at[slot, rows_of(c)],
            send_sem=send_sem,
            recv_sem=ag_recv.at[slot, c],
            device_id=device_id,
            device_id_type=MESH,
        )

    def own_to_left(c):
        return send_block(mem_all.at[own_slot, rows_of(c)], own_slot, c, ag_own_send.at[0, c], {"mp": z - 1})

    def own_to_right(c):
        return send_block(mem_all.at[own_slot, rows_of(c)], own_slot, c, ag_own_send.at[1, c], {"mp": z + 1})

    def to_x(k, c):
        slot = x * n + near[k]
        return send_block(mem_all.at[slot, rows_of(c)], slot, c, ag_x_send.at[k, c], {"section": other})

    def relay(k, c):
        slot = x * n + near[k]
        dest = jnp.where(near[k] < z, z + 1, z - 1)
        return send_block(mem_all.at[slot, rows_of(c)], slot, c, ag_z_send.at[k, c], {"mp": dest})

    def relays(k):
        j = near[k]
        return ((j < z) & (z < n - 1)) | ((j > z) & (z > 0))

    def arrived(slot, c):
        send_block(mem_all.at[slot, rows_of(c)], slot, c, ag_x_send.at[0, c], {"section": other}).wait_recv()

    def send_own():
        for c in range(CHUNKS):

            @pl.when(z > 0)
            def _():
                own_to_left(c).start()

            @pl.when(z < n - 1)
            def _():
                own_to_right(c).start()

            to_x(0, c).start()

    def send_length(r):
        peer = lax.rem(dp + r, n_dp)
        return pltpu.make_async_remote_copy(
            src_ref=len_own,
            dst_ref=len_all.at[dp],
            send_sem=len_send.at[r],
            recv_sem=len_recv.at[dp],
            device_id={"dp": peer},
            device_id_type=MESH,
        )

    for r in range(1, n_dp):
        send_length(r).start()
    loads[0].wait()

    paired = n_dp % 2 == 0
    first = (lax.rem(dp, 2) == 1) if paired else True
    if paired:
        pl.when(first)(send_own)
    else:
        send_own()
    loads[1].wait()
    q_t[...] = q[...].T
    k_acc[...] = jnp.zeros_like(k_acc)
    v_acc[...] = jnp.zeros_like(v_acc)
    if paired:

        @pl.when(jnp.logical_not(first))
        def _():
            pl.semaphore_wait(turn_sem, 1)
            send_own()

    valid = (
        lax.broadcasted_iota(jnp.int32, (seq_rows, 1), 0) < length
    ).astype(jnp.float32)
    for k in range(1, n):
        for c in range(CHUNKS):
            arrived(x * n + near[k], c)

            @pl.when(relays(k))
            def _():
                relay(k, c).start()

            to_x(k, c).start()
        if paired and k == min(TURN_AT, n - 1):

            @pl.when(first)
            def _():
                pl.semaphore_signal(turn_sem, inc=1, device_id={"dp": dp - 1}, device_id_type=MESH)

    total = len_own[...]
    for r in range(1, n_dp):
        peer = lax.rem(dp + r, n_dp)
        pltpu.make_async_remote_copy(
            src_ref=len_own,
            dst_ref=len_all.at[peer],
            send_sem=len_send.at[r],
            recv_sem=len_recv.at[peer],
            device_id={"dp": peer},
            device_id_type=MESH,
        ).wait_recv()
        total = total + len_all[peer]
    loss_weight = (float(n_dp * seq_rows) / total)[0:1, 0:1]
    loads[2].wait()
    weighted = (cot[...].astype(jnp.float32) * (valid * loss_weight)).astype(jnp.bfloat16)
    w[...] = weighted
    w_t[...] = weighted.T
    loads[3].wait()
    loads[4].wait()

    @pl.loop(0, 2 * n)
    def _(e):
        own_row = e < n
        slot = jnp.where(own_row, x * n, other * n) + pick(near, jnp.where(own_row, e, e - n))

        @pl.when(e >= n)
        def _():
            for c in range(CHUNKS):
                arrived(slot, c)

        rows = pl.ds(pl.multiple_of(slot * block, block), block)
        mem_block = mem_all[slot]
        k_acc[...] += jnp.dot(mem_block, kw[rows, :], preferred_element_type=jnp.float32)
        v_acc[...] += jnp.dot(mem_block, vw[rows, :], preferred_element_type=jnp.float32)

    last = (((1,), (1,)), ((), ()))

    @pl.loop(0, heads)
    def _(h):
        cols = pl.ds(pl.multiple_of(h * HEAD_DIM, HEAD_DIM), HEAD_DIM)
        key_h = k_acc[:, cols].astype(jnp.bfloat16)
        value_h = v_acc[:, cols].astype(jnp.bfloat16)
        scores = (
            lax.dot_general(q[:, cols], key_h, last, preferred_element_type=jnp.float32)
            * score_scale
        )
        prob_grad = lax.dot_general(w[:, cols], value_h, last, preferred_element_type=jnp.float32)
        top = jnp.max(scores, axis=-1, keepdims=True)
        powers = jnp.exp(scores - top)
        attention = powers * (1.0 / jnp.sum(powers, axis=-1, keepdims=True))
        attention_low = attention.astype(jnp.bfloat16)
        row_dot = jnp.sum(attention * prob_grad, axis=-1, keepdims=True)
        score_grad = (attention * (prob_grad - row_dot) * score_scale).astype(jnp.bfloat16)
        dv_t[cols, :] = jnp.dot(
            w_t[cols, :], attention_low, preferred_element_type=jnp.float32
        ).astype(jnp.bfloat16)
        dk_t[cols, :] = jnp.dot(
            q_t[cols, :], score_grad, preferred_element_type=jnp.float32
        ).astype(jnp.bfloat16)
        context = jnp.dot(attention_low, value_h, preferred_element_type=jnp.float32)
        ctx[:, cols] = (context * valid).astype(jnp.bfloat16)
    ctx_copy = pltpu.make_async_copy(ctx, ctx_out, local_sem.at[0])
    ctx_copy.start()

    def feats_of(c):
        return pl.ds(c * part_feats, part_feats)

    def sum_to_x(j, c):
        return pltpu.make_async_remote_copy(
            src_ref=xs.at[j, feats_of(c)],
            dst_ref=xr.at[j, feats_of(c)],
            send_sem=rs_x_send.at[j, c],
            recv_sem=rs_x_recv.at[j, c],
            device_id={"section": other},
            device_id_type=MESH,
        )

    def sum_along_z(j, c, slot):
        dest = jnp.where(j > z, z + 1, z - 1)
        return pltpu.make_async_remote_copy(
            src_ref=zs.at[j, feats_of(c)],
            dst_ref=zr.at[slot, feats_of(c)],
            send_sem=rs_z_send.at[j, c],
            recv_sem=rs_z_recv.at[slot, c],
            device_id={"mp": dest},
            device_id_type=MESH,
        )

    @pl.loop(0, 2 * n)
    def _(e):
        sent = e < n
        j = pick(far, jnp.where(sent, e, e - n))
        slot = jnp.where(sent, other * n, x * n) + j
        rows = pl.ds(pl.multiple_of(slot * block, block), block)
        acc[j] = jnp.dot(
            kw[rows, :], dk_t[...], preferred_element_type=jnp.float32
        ) + jnp.dot(vw[rows, :], dv_t[...], preferred_element_type=jnp.float32)

        @pl.when(sent)
        def _():
            xs[j] = acc[j].astype(jnp.bfloat16)
            for c in range(CHUNKS):
                sum_to_x(j, c).start()

    def target_slot(j):
        return jnp.where((j < z) & (z - 1 == j), n, j)

    @pl.loop(0, n - 1)
    def _(k):
        j = pick(far, k)
        has_source = ((j > z) & (z > 0)) | ((j < z) & (z < n - 1))
        for c in range(CHUNKS):
            sum_to_x(j, c).wait_recv()
            acc[j, feats_of(c)] += xr[j, feats_of(c)].astype(jnp.float32)

            @pl.when(has_source)
            def _():
                sum_along_z(j, c, j).wait_recv()
                acc[j, feats_of(c)] += zr[j, feats_of(c)].astype(jnp.float32)

            zs[j, feats_of(c)] = acc[j, feats_of(c)].astype(jnp.bfloat16)
            sum_along_z(j, c, target_slot(j)).start()

    for c in range(CHUNKS):
        sum_to_x(z, c).wait_recv()
        grad_out[feats_of(c)] = acc[z, feats_of(c)] + xr[z, feats_of(c)].astype(jnp.float32)

        @pl.when(z > 0)
        def _():
            sum_along_z(far[0], c, z).wait_recv()
            grad_out[feats_of(c)] += zr[z, feats_of(c)].astype(jnp.float32)

        @pl.when(z < n - 1)
        def _():
            sum_along_z(far[0], c, n).wait_recv()
            grad_out[feats_of(c)] += zr[n, feats_of(c)].astype(jnp.float32)

    for c in range(CHUNKS):

        @pl.when(z > 0)
        def _():
            own_to_left(c).wait_send()

        @pl.when(z < n - 1)
        def _():
            own_to_right(c).wait_send()

        for k in range(n):
            to_x(k, c).wait_send()
            sum_to_x(far[k], c).wait_send()
        for k in range(1, n):

            @pl.when(relays(k))
            def _():
                relay(k, c).wait_send()

        for k in range(n - 1):
            sum_along_z(far[k], c, target_slot(far[k])).wait_send()
    for r in range(1, n_dp):
        send_length(r).wait_send()
    ctx_copy.wait()


def fused(n, n_dp, memory, key_weight, value_weight, queries, cotangent, target_lengths):
    mem_rows, block = memory.shape[1:]
    feats, width = key_weight.shape[1:]
    seq_rows = queries.shape[2]
    low, full = jnp.bfloat16, jnp.float32
    vmem, sem = pltpu.VMEM, pltpu.SemaphoreType.DMA
    anywhere = pl.BlockSpec(memory_space=pl.ANY)
    context, grad = pl.pallas_call(
        functools.partial(fused_kernel, n, n_dp),
        out_shape=(
            jax.ShapeDtypeStruct((seq_rows, width), low),
            jax.ShapeDtypeStruct((block, mem_rows), full),
        ),
        in_specs=[pl.BlockSpec(memory_space=pltpu.SMEM)] + [anywhere] * 5,
        out_specs=(anywhere, pl.BlockSpec(memory_space=pltpu.VMEM)),
        scratch_shapes=[
            vmem((feats, width), low),
            vmem((feats, width), low),
            vmem((seq_rows, width), low),
            vmem((seq_rows, width), low),
            vmem((2 * n, mem_rows, block), low),
            vmem((mem_rows, width), full),
            vmem((mem_rows, width), full),
            vmem((width, seq_rows), low),
            vmem((seq_rows, width), low),
            vmem((width, seq_rows), low),
            vmem((seq_rows, width), low),
            vmem((width, mem_rows), low),
            vmem((width, mem_rows), low),
            vmem((n, block, mem_rows), low),
            vmem((n, block, mem_rows), low),
            vmem((n, block, mem_rows), full),
            vmem((n, block, mem_rows), low),
            vmem((n + 1, block, mem_rows), low),
            vmem((8, 128), full),
            vmem((n_dp, 8, 128), full),
            sem((5,)),
            sem((2, CHUNKS)),
            sem((n, CHUNKS)),
            sem((n, CHUNKS)),
            sem((2 * n, CHUNKS)),
            sem((n, CHUNKS)),
            sem((n, CHUNKS)),
            sem((n, CHUNKS)),
            sem((n + 1, CHUNKS)),
            sem((n_dp,)),
            sem((n_dp,)),
            pltpu.SemaphoreType.REGULAR,
        ],
        compiler_params=pltpu.CompilerParams(
            collective_id=0, has_side_effects=True, vmem_limit_bytes=60 * 1024 * 1024
        ),
    )(
        target_lengths,
        memory[0],
        key_weight[0],
        value_weight[0],
        queries[0, 0],
        cotangent[0, 0],
    )
    context, grad = pl.pallas_call(
        finish_kernel,
        out_shape=(
            jax.ShapeDtypeStruct((seq_rows, width), low),
            jax.ShapeDtypeStruct((mem_rows, block), full),
        ),
        in_specs=[anywhere] * 2,
        out_specs=(anywhere, anywhere),
        scratch_shapes=[
            vmem((seq_rows, width), low),
            vmem((block, mem_rows), full),
            vmem((mem_rows, block), full),
            sem((4,)),
        ],
        compiler_params=pltpu.CompilerParams(vmem_limit_bytes=60 * 1024 * 1024),
    )(context, grad)
    return context[None, None], grad[None]


def on_device(memory, key_weight, value_weight, queries, cotangent, target_lengths):
    width = key_weight.shape[2]
    head_count = width // HEAD_DIM
    seq_rows = queries.shape[2]
    score_scale = HEAD_DIM ** (-0.5)
    mem_block = memory[0]
    mem_rows = mem_block.shape[0]
    full_memory = lax.all_gather(mem_block, ("section", "mp"), axis=1, tiled=True)
    token_total = lax.psum(target_lengths.astype(jnp.float32), "dp")
    slot_total = float(lax.axis_size("dp") * target_lengths.shape[0] * seq_rows)
    loss_weight = slot_total / token_total[0]
    valid = (jnp.arange(seq_rows, dtype=jnp.int32) < target_lengths[0]).astype(jnp.float32)
    layer_index = 0
    key_rows = jnp.dot(
        full_memory, key_weight[layer_index], preferred_element_type=jnp.float32
    ).astype(jnp.bfloat16)
    value_rows = jnp.dot(
        full_memory, value_weight[layer_index], preferred_element_type=jnp.float32
    ).astype(jnp.bfloat16)
    key_heads = key_rows.reshape(mem_rows, head_count, HEAD_DIM)
    value_heads = value_rows.reshape(mem_rows, head_count, HEAD_DIM)
    query_heads = queries[layer_index, 0].reshape(seq_rows, head_count, HEAD_DIM)
    scores = (
        jnp.einsum("thd,shd->hts", query_heads, key_heads, preferred_element_type=jnp.float32)
        * score_scale
    )
    attention = jax.nn.softmax(scores, axis=-1)
    attention_low = attention.astype(jnp.bfloat16)
    context = jnp.einsum(
        "hts,shd->thd", attention_low, value_heads, preferred_element_type=jnp.float32
    )
    context = (context * valid[:, None, None]).astype(jnp.bfloat16)
    contexts = [context.reshape(seq_rows, width)]
    weighted = cotangent[layer_index, 0].astype(jnp.float32) * (valid * loss_weight)[:, None]
    weighted = weighted.astype(jnp.bfloat16).reshape(seq_rows, head_count, HEAD_DIM)
    value_grad = jnp.einsum(
        "hts,thd->shd", attention_low, weighted, preferred_element_type=jnp.float32
    )
    value_grads = [value_grad.astype(jnp.bfloat16).reshape(mem_rows, width)]
    prob_grad = jnp.einsum(
        "thd,shd->hts", weighted, value_heads, preferred_element_type=jnp.float32
    )
    row_dot = jnp.sum(attention * prob_grad, axis=-1, keepdims=True)
    score_grad = (attention * (prob_grad - row_dot) * score_scale).astype(jnp.bfloat16)
    key_grad = jnp.einsum(
        "hts,thd->shd", score_grad, query_heads, preferred_element_type=jnp.float32
    )
    key_grads = [key_grad.astype(jnp.bfloat16).reshape(mem_rows, width)]
    contract_last = (((1,), (1,)), ((), ()))
    layer_index = 0
    key_part = key_weight[layer_index]
    value_part = value_weight[layer_index]
    running = lax.dot_general(
        key_part, key_grads[layer_index], contract_last, preferred_element_type=jnp.float32
    )
    running = running + lax.dot_general(
        value_part, value_grads[layer_index], contract_last, preferred_element_type=jnp.float32
    )
    section_part = lax.psum_scatter(
        running.astype(jnp.bfloat16), "section", scatter_dimension=0, tiled=True
    )
    own_part = lax.psum_scatter(section_part, "mp", scatter_dimension=0, tiled=True).astype(
        jnp.float32
    )
    own_grad = own_part.T
    context_out = jnp.stack(contexts, axis=0)[:, None]
    return (context_out, own_grad[None])


def solution(mesh):
    sections, n, n_dp = mesh.shape["section"], mesh.shape["mp"], mesh.shape["dp"]

    def per_device(memory, key_weight, value_weight, queries, cotangent, target_lengths):
        args = (memory, key_weight, value_weight, queries, cotangent, target_lengths)
        mem_rows, block = memory.shape[1:]
        if sections == 2 and n >= 2 and mem_rows % 128 == 0 and block % 128 == 0:
            return fused(n, n_dp, *args)
        return on_device(*args)

    return jax.shard_map(
        per_device,
        mesh=mesh,
        in_specs=(
            P("dp", None, ("section", "mp")),
            P("section", None, "mp"),
            P("section", None, "mp"),
            P("section", "dp", None, "mp"),
            P("section", "dp", None, "mp"),
            P("dp"),
        ),
        out_specs=(P("section", "dp", None, "mp"), P("dp", None, ("section", "mp"))),
        check_vma=False,
    )
```

```python
import functools

import jax
import jax.numpy as jnp
from jax import lax
from jax.experimental import pallas as pl
from jax.experimental.pallas import tpu as pltpu
from jax.sharding import PartitionSpec as P

HEAD_DIM = 256
CHUNKS = 2
REACH = 2
MESH = pl.DeviceIdType.MESH


def far_to_near(z, n):
    low, high, order = 0, n - 1, []
    for _ in range(n):
        take_low = (z - low) >= (high - z)
        order.append(jnp.where(take_low, low, high))
        low, high = jnp.where(take_low, low + 1, low), jnp.where(take_low, high, high - 1)
    return order


def pick(order, at):
    found = order[0]
    for i in range(1, len(order)):
        found = jnp.where(at == i, order[i], found)
    return found


def finish_kernel(ctx_ref, grad_ref, ctx_out, grad_out, ctx, grad, grad_t, sems):
    grad_load = pltpu.make_async_copy(grad_ref, grad, sems.at[0])
    ctx_load = pltpu.make_async_copy(ctx_ref, ctx, sems.at[1])
    grad_load.start()
    ctx_load.start()
    grad_load.wait()
    grad_t[...] = grad[...].T
    grad_store = pltpu.make_async_copy(grad_t, grad_out, sems.at[2])
    grad_store.start()
    ctx_load.wait()
    ctx_store = pltpu.make_async_copy(ctx, ctx_out, sems.at[3])
    ctx_store.start()
    grad_store.wait()
    ctx_store.wait()


def fused_kernel(
    n, n_dp,
    len_ref, memory_ref, kw_ref, vw_ref, q_ref, cot_ref,
    ctx_out, grad_out,
    kw, vw, q, cot, mem_all, k_acc, v_acc, q_t, w, w_t, ctx, dk_t, dv_t,
    xs, xr, acc, zs, zr, len_own, len_all,
    local_sem, ag_own_send, ag_z_send, ag_x_send, ag_recv,
    rs_x_send, rs_x_recv, rs_z_send, rs_z_recv, len_send, len_recv,
):
    x = lax.axis_index("section")
    z = lax.axis_index("mp")
    dp = lax.axis_index("dp")
    other = 1 - x
    mem_rows, block = memory_ref.shape
    seq_rows, width = q_ref.shape
    heads = width // HEAD_DIM
    score_scale = HEAD_DIM ** (-0.5)
    part_rows = mem_rows // CHUNKS
    part_feats = block // CHUNKS
    far = far_to_near(z, n)
    near = far[::-1]

    own_slot = x * n + z
    loads = [
        pltpu.make_async_copy(src, dst, local_sem.at[i])
        for i, (src, dst) in enumerate(
            (
                (memory_ref, mem_all.at[own_slot]),
                (q_ref, q),
                (cot_ref, cot),
                (kw_ref, kw),
                (vw_ref, vw),
            )
        )
    ]
    for load in loads:
        load.start()
    length = len_ref[0]
    len_own[...] = jnp.full(len_own.shape, length.astype(jnp.float32), jnp.float32)

    barrier = pltpu.get_barrier_semaphore()
    pl.semaphore_signal(barrier, inc=1, device_id={"section": other}, device_id_type=MESH)
    for r in range(1, n_dp):
        peer = lax.rem(dp + r, n_dp)
        pl.semaphore_signal(barrier, inc=1, device_id={"dp": peer}, device_id_type=MESH)

    line_peers = 0
    for step in range(1, min(REACH, n - 1) + 1):

        @pl.when(z - step >= 0)
        def _():
            pl.semaphore_signal(barrier, inc=1, device_id={"mp": z - step}, device_id_type=MESH)

        @pl.when(z + step < n)
        def _():
            pl.semaphore_signal(barrier, inc=1, device_id={"mp": z + step}, device_id_type=MESH)

        line_peers += jnp.where(z - step >= 0, 1, 0) + jnp.where(z + step < n, 1, 0)
    pl.semaphore_wait(barrier, n_dp + line_peers)

    def distance(j):
        return jnp.where(j > z, j - z, z - j)

    def rows_of(c):
        return pl.ds(c * part_rows, part_rows)

    def send_block(src, slot, c, send_sem, device_id):
        return pltpu.make_async_remote_copy(
            src_ref=src,
            dst_ref=mem_all.at[slot, rows_of(c)],
            send_sem=send_sem,
            recv_sem=ag_recv.at[slot, c],
            device_id=device_id,
            device_id_type=MESH,
        )

    def to_line(k, c):
        return send_block(
            mem_all.at[own_slot, rows_of(c)], own_slot, c, ag_own_send.at[k, c], {"mp": near[k]}
        )

    def to_x(k, c):
        slot = x * n + near[k]
        return send_block(mem_all.at[slot, rows_of(c)], slot, c, ag_x_send.at[k, c], {"section": other})

    def relay(k, c):
        slot = x * n + near[k]
        dest = jnp.where(near[k] < z, z + 1, z - 1)
        return send_block(mem_all.at[slot, rows_of(c)], slot, c, ag_z_send.at[k, c], {"mp": dest})

    def relays(k):
        j = near[k]
        return (distance(j) >= REACH) & (((j < z) & (z < n - 1)) | ((j > z) & (z > 0)))

    def arrived(slot, c):
        send_block(mem_all.at[slot, rows_of(c)], slot, c, ag_x_send.at[0, c], {"section": other}).wait_recv()

    def reached(j):
        return distance(j) <= REACH

    def send_length(r):
        peer = lax.rem(dp + r, n_dp)
        return pltpu.make_async_remote_copy(
            src_ref=len_own,
            dst_ref=len_all.at[dp],
            send_sem=len_send.at[r],
            recv_sem=len_recv.at[dp],
            device_id={"dp": peer},
            device_id_type=MESH,
        )

    for r in range(1, n_dp):
        send_length(r).start()
    loads[0].wait()

    for c in range(CHUNKS):
        to_line(1, c).start()
        to_x(0, c).start()
    for k in range(2, n):
        for c in range(CHUNKS):

            @pl.when(reached(near[k]))
            def _():
                to_line(k, c).start()

    loads[1].wait()
    q_t[...] = q[...].T
    k_acc[...] = jnp.zeros_like(k_acc)
    v_acc[...] = jnp.zeros_like(v_acc)
    valid = (
        lax.broadcasted_iota(jnp.int32, (seq_rows, 1), 0) < length
    ).astype(jnp.float32)
    for k in range(1, n):
        for c in range(CHUNKS):
            arrived(x * n + near[k], c)

            @pl.when(relays(k))
            def _():
                relay(k, c).start()

            to_x(k, c).start()

    total = len_own[...]
    for r in range(1, n_dp):
        peer = lax.rem(dp + r, n_dp)
        pltpu.make_async_remote_copy(
            src_ref=len_own,
            dst_ref=len_all.at[peer],
            send_sem=len_send.at[r],
            recv_sem=len_recv.at[peer],
            device_id={"dp": peer},
            device_id_type=MESH,
        ).wait_recv()
        total = total + len_all[peer]
    loss_weight = (float(n_dp * seq_rows) / total)[0:1, 0:1]
    loads[2].wait()
    weighted = (cot[...].astype(jnp.float32) * (valid * loss_weight)).astype(jnp.bfloat16)
    w[...] = weighted
    w_t[...] = weighted.T
    loads[3].wait()
    loads[4].wait()

    @pl.loop(0, 2 * n)
    def _(e):
        own_row = e < n
        slot = jnp.where(own_row, x * n, other * n) + pick(near, jnp.where(own_row, e, e - n))

        @pl.when(e >= n)
        def _():
            for c in range(CHUNKS):
                arrived(slot, c)

        rows = pl.ds(pl.multiple_of(slot * block, block), block)
        mem_block = mem_all[slot]
        k_acc[...] += jnp.dot(mem_block, kw[rows, :], preferred_element_type=jnp.float32)
        v_acc[...] += jnp.dot(mem_block, vw[rows, :], preferred_element_type=jnp.float32)

    last = (((1,), (1,)), ((), ()))

    @pl.loop(0, heads)
    def _(h):
        cols = pl.ds(pl.multiple_of(h * HEAD_DIM, HEAD_DIM), HEAD_DIM)
        key_h = k_acc[:, cols].astype(jnp.bfloat16)
        value_h = v_acc[:, cols].astype(jnp.bfloat16)
        scores = (
            lax.dot_general(q[:, cols], key_h, last, preferred_element_type=jnp.float32)
            * score_scale
        )
        prob_grad = lax.dot_general(w[:, cols], value_h, last, preferred_element_type=jnp.float32)
        top = jnp.max(scores, axis=-1, keepdims=True)
        powers = jnp.exp(scores - top)
        attention = powers * (1.0 / jnp.sum(powers, axis=-1, keepdims=True))
        attention_low = attention.astype(jnp.bfloat16)
        row_dot = jnp.sum(attention * prob_grad, axis=-1, keepdims=True)
        score_grad = (attention * (prob_grad - row_dot) * score_scale).astype(jnp.bfloat16)
        dv_t[cols, :] = jnp.dot(
            w_t[cols, :], attention_low, preferred_element_type=jnp.float32
        ).astype(jnp.bfloat16)
        dk_t[cols, :] = jnp.dot(
            q_t[cols, :], score_grad, preferred_element_type=jnp.float32
        ).astype(jnp.bfloat16)
        context = jnp.dot(attention_low, value_h, preferred_element_type=jnp.float32)
        ctx[:, cols] = (context * valid).astype(jnp.bfloat16)
    ctx_copy = pltpu.make_async_copy(ctx, ctx_out, local_sem.at[0])
    ctx_copy.start()

    def feats_of(c):
        return pl.ds(c * part_feats, part_feats)

    def sum_to_x(j, c):
        return pltpu.make_async_remote_copy(
            src_ref=xs.at[j, feats_of(c)],
            dst_ref=xr.at[j, feats_of(c)],
            send_sem=rs_x_send.at[j, c],
            recv_sem=rs_x_recv.at[j, c],
            device_id={"section": other},
            device_id_type=MESH,
        )

    def sum_along_z(j, c, slot):
        far_off = distance(j) > REACH
        step = jnp.where(j > z, z + 1, z - 1)
        return pltpu.make_async_remote_copy(
            src_ref=zs.at[j, feats_of(c)],
            dst_ref=zr.at[slot, feats_of(c)],
            send_sem=rs_z_send.at[j, c],
            recv_sem=rs_z_recv.at[slot, c],
            device_id={"mp": jnp.where(far_off, step, j)},
            device_id_type=MESH,
        )

    @pl.loop(0, 2 * n)
    def _(e):
        sent = e < n
        j = pick(far, jnp.where(sent, e, e - n))
        slot = jnp.where(sent, other * n, x * n) + j
        rows = pl.ds(pl.multiple_of(slot * block, block), block)
        acc[j] = jnp.dot(
            kw[rows, :], dk_t[...], preferred_element_type=jnp.float32
        ) + jnp.dot(vw[rows, :], dv_t[...], preferred_element_type=jnp.float32)

        @pl.when(sent)
        def _():
            xs[j] = acc[j].astype(jnp.bfloat16)
            for c in range(CHUNKS):
                sum_to_x(j, c).start()

    def target_slot(j):
        return jnp.where(distance(j) > REACH, n + j, z)

    @pl.loop(0, n - 1)
    def _(k):
        j = pick(far, k)
        has_source = (distance(j) >= REACH) & (
            ((j > z) & (z > 0)) | ((j < z) & (z < n - 1))
        )
        for c in range(CHUNKS):
            sum_to_x(j, c).wait_recv()
            acc[j, feats_of(c)] += xr[j, feats_of(c)].astype(jnp.float32)

            @pl.when(has_source)
            def _():
                sum_along_z(j, c, n + j).wait_recv()
                acc[j, feats_of(c)] += zr[n + j, feats_of(c)].astype(jnp.float32)

            zs[j, feats_of(c)] = acc[j, feats_of(c)].astype(jnp.bfloat16)
            sum_along_z(j, c, target_slot(j)).start()

    for c in range(CHUNKS):
        sum_to_x(z, c).wait_recv()
        grad_out[feats_of(c)] = acc[z, feats_of(c)] + xr[z, feats_of(c)].astype(jnp.float32)

        for k in range(1, n):

            @pl.when(reached(near[k]))
            def _():
                sum_along_z(near[k], c, near[k]).wait_recv()
                grad_out[feats_of(c)] += zr[near[k], feats_of(c)].astype(jnp.float32)

    for c in range(CHUNKS):
        for k in range(n):
            to_x(k, c).wait_send()
            sum_to_x(far[k], c).wait_send()
        for k in range(1, n):

            @pl.when(reached(near[k]))
            def _():
                to_line(k, c).wait_send()

            @pl.when(relays(k))
            def _():
                relay(k, c).wait_send()

        for k in range(n - 1):
            sum_along_z(far[k], c, target_slot(far[k])).wait_send()
    for r in range(1, n_dp):
        send_length(r).wait_send()
    ctx_copy.wait()


def fused(n, n_dp, memory, key_weight, value_weight, queries, cotangent, target_lengths):
    mem_rows, block = memory.shape[1:]
    feats, width = key_weight.shape[1:]
    seq_rows = queries.shape[2]
    low, full = jnp.bfloat16, jnp.float32
    vmem, sem = pltpu.VMEM, pltpu.SemaphoreType.DMA
    anywhere = pl.BlockSpec(memory_space=pl.ANY)
    context, grad = pl.pallas_call(
        functools.partial(fused_kernel, n, n_dp),
        out_shape=(
            jax.ShapeDtypeStruct((seq_rows, width), low),
            jax.ShapeDtypeStruct((block, mem_rows), full),
        ),
        in_specs=[pl.BlockSpec(memory_space=pltpu.SMEM)] + [anywhere] * 5,
        out_specs=(anywhere, pl.BlockSpec(memory_space=pltpu.VMEM)),
        scratch_shapes=[
            vmem((feats, width), low),
            vmem((feats, width), low),
            vmem((seq_rows, width), low),
            vmem((seq_rows, width), low),
            vmem((2 * n, mem_rows, block), low),
            vmem((mem_rows, width), full),
            vmem((mem_rows, width), full),
            vmem((width, seq_rows), low),
            vmem((seq_rows, width), low),
            vmem((width, seq_rows), low),
            vmem((seq_rows, width), low),
            vmem((width, mem_rows), low),
            vmem((width, mem_rows), low),
            vmem((n, block, mem_rows), low),
            vmem((n, block, mem_rows), low),
            vmem((n, block, mem_rows), full),
            vmem((n, block, mem_rows), low),
            vmem((2 * n, block, mem_rows), low),
            vmem((8, 128), full),
            vmem((n_dp, 8, 128), full),
            sem((5,)),
            sem((n, CHUNKS)),
            sem((n, CHUNKS)),
            sem((n, CHUNKS)),
            sem((2 * n, CHUNKS)),
            sem((n, CHUNKS)),
            sem((n, CHUNKS)),
            sem((n, CHUNKS)),
            sem((2 * n, CHUNKS)),
            sem((n_dp,)),
            sem((n_dp,)),
        ],
        compiler_params=pltpu.CompilerParams(
            collective_id=0, has_side_effects=True, vmem_limit_bytes=60 * 1024 * 1024
        ),
    )(
        target_lengths,
        memory[0],
        key_weight[0],
        value_weight[0],
        queries[0, 0],
        cotangent[0, 0],
    )
    context, grad = pl.pallas_call(
        finish_kernel,
        out_shape=(
            jax.ShapeDtypeStruct((seq_rows, width), low),
            jax.ShapeDtypeStruct((mem_rows, block), full),
        ),
        in_specs=[anywhere] * 2,
        out_specs=(anywhere, anywhere),
        scratch_shapes=[
            vmem((seq_rows, width), low),
            vmem((block, mem_rows), full),
            vmem((mem_rows, block), full),
            sem((4,)),
        ],
        compiler_params=pltpu.CompilerParams(vmem_limit_bytes=60 * 1024 * 1024),
    )(context, grad)
    return context[None, None], grad[None]


def on_device(memory, key_weight, value_weight, queries, cotangent, target_lengths):
    width = key_weight.shape[2]
    head_count = width // HEAD_DIM
    seq_rows = queries.shape[2]
    score_scale = HEAD_DIM ** (-0.5)
    mem_block = memory[0]
    mem_rows = mem_block.shape[0]
    full_memory = lax.all_gather(mem_block, ("section", "mp"), axis=1, tiled=True)
    token_total = lax.psum(target_lengths.astype(jnp.float32), "dp")
    slot_total = float(lax.axis_size("dp") * target_lengths.shape[0] * seq_rows)
    loss_weight = slot_total / token_total[0]
    valid = (jnp.arange(seq_rows, dtype=jnp.int32) < target_lengths[0]).astype(jnp.float32)
    layer_index = 0
    key_rows = jnp.dot(
        full_memory, key_weight[layer_index], preferred_element_type=jnp.float32
    ).astype(jnp.bfloat16)
    value_rows = jnp.dot(
        full_memory, value_weight[layer_index], preferred_element_type=jnp.float32
    ).astype(jnp.bfloat16)
    key_heads = key_rows.reshape(mem_rows, head_count, HEAD_DIM)
    value_heads = value_rows.reshape(mem_rows, head_count, HEAD_DIM)
    query_heads = queries[layer_index, 0].reshape(seq_rows, head_count, HEAD_DIM)
    scores = (
        jnp.einsum("thd,shd->hts", query_heads, key_heads, preferred_element_type=jnp.float32)
        * score_scale
    )
    attention = jax.nn.softmax(scores, axis=-1)
    attention_low = attention.astype(jnp.bfloat16)
    context = jnp.einsum(
        "hts,shd->thd", attention_low, value_heads, preferred_element_type=jnp.float32
    )
    context = (context * valid[:, None, None]).astype(jnp.bfloat16)
    contexts = [context.reshape(seq_rows, width)]
    weighted = cotangent[layer_index, 0].astype(jnp.float32) * (valid * loss_weight)[:, None]
    weighted = weighted.astype(jnp.bfloat16).reshape(seq_rows, head_count, HEAD_DIM)
    value_grad = jnp.einsum(
        "hts,thd->shd", attention_low, weighted, preferred_element_type=jnp.float32
    )
    value_grads = [value_grad.astype(jnp.bfloat16).reshape(mem_rows, width)]
    prob_grad = jnp.einsum(
        "thd,shd->hts", weighted, value_heads, preferred_element_type=jnp.float32
    )
    row_dot = jnp.sum(attention * prob_grad, axis=-1, keepdims=True)
    score_grad = (attention * (prob_grad - row_dot) * score_scale).astype(jnp.bfloat16)
    key_grad = jnp.einsum(
        "hts,thd->shd", score_grad, query_heads, preferred_element_type=jnp.float32
    )
    key_grads = [key_grad.astype(jnp.bfloat16).reshape(mem_rows, width)]
    contract_last = (((1,), (1,)), ((), ()))
    layer_index = 0
    key_part = key_weight[layer_index]
    value_part = value_weight[layer_index]
    running = lax.dot_general(
        key_part, key_grads[layer_index], contract_last, preferred_element_type=jnp.float32
    )
    running = running + lax.dot_general(
        value_part, value_grads[layer_index], contract_last, preferred_element_type=jnp.float32
    )
    section_part = lax.psum_scatter(
        running.astype(jnp.bfloat16), "section", scatter_dimension=0, tiled=True
    )
    own_part = lax.psum_scatter(section_part, "mp", scatter_dimension=0, tiled=True).astype(
        jnp.float32
    )
    own_grad = own_part.T
    context_out = jnp.stack(contexts, axis=0)[:, None]
    return (context_out, own_grad[None])


def solution(mesh):
    sections, n, n_dp = mesh.shape["section"], mesh.shape["mp"], mesh.shape["dp"]

    def per_device(memory, key_weight, value_weight, queries, cotangent, target_lengths):
        args = (memory, key_weight, value_weight, queries, cotangent, target_lengths)
        mem_rows, block = memory.shape[1:]
        if sections == 2 and n >= 2 and mem_rows % 128 == 0 and block % 128 == 0:
            return fused(n, n_dp, *args)
        return on_device(*args)

    return jax.shard_map(
        per_device,
        mesh=mesh,
        in_specs=(
            P("dp", None, ("section", "mp")),
            P("section", None, "mp"),
            P("section", None, "mp"),
            P("section", "dp", None, "mp"),
            P("section", "dp", None, "mp"),
            P("dp"),
        ),
        out_specs=(P("section", "dp", None, "mp"), P("dp", None, ("section", "mp"))),
        check_vma=False,
    )
```

```python
import functools

import jax
import jax.numpy as jnp
from jax import lax
from jax.experimental import pallas as pl
from jax.experimental.pallas import tpu as pltpu
from jax.sharding import PartitionSpec as P

HEAD_DIM = 256
CHUNKS = 2
REACH = 2
MESH = pl.DeviceIdType.MESH


def far_to_near(z, n):
    low, high, order = 0, n - 1, []
    for _ in range(n):
        take_low = (z - low) >= (high - z)
        order.append(jnp.where(take_low, low, high))
        low, high = jnp.where(take_low, low + 1, low), jnp.where(take_low, high, high - 1)
    return order


def pick(order, at):
    found = order[0]
    for i in range(1, len(order)):
        found = jnp.where(at == i, order[i], found)
    return found


def finish_kernel(ctx_ref, grad_ref, ctx_out, grad_out, ctx, grad, grad_t, sems):
    grad_load = pltpu.make_async_copy(grad_ref, grad, sems.at[0])
    ctx_load = pltpu.make_async_copy(ctx_ref, ctx, sems.at[1])
    grad_load.start()
    ctx_load.start()
    grad_load.wait()
    grad_t[...] = grad[...].T
    grad_store = pltpu.make_async_copy(grad_t, grad_out, sems.at[2])
    grad_store.start()
    ctx_load.wait()
    ctx_store = pltpu.make_async_copy(ctx, ctx_out, sems.at[3])
    ctx_store.start()
    grad_store.wait()
    ctx_store.wait()


def fused_kernel(
    n, n_dp,
    len_ref, memory_ref, kw_ref, vw_ref, q_ref, cot_ref,
    ctx_out, grad_out,
    kw, vw, q, cot, mem_all, k_acc, v_acc, q_t, w, w_t, ctx, dk_t, dv_t,
    xs, xr, acc, zs, zr, len_own, len_all,
    local_sem, ag_own_send, ag_z_send, ag_x_send, ag_recv,
    rs_x_send, rs_x_recv, rs_z_send, rs_z_recv, len_send, len_recv,
):
    x = lax.axis_index("section")
    z = lax.axis_index("mp")
    dp = lax.axis_index("dp")
    other = 1 - x
    mem_rows, block = memory_ref.shape
    seq_rows, width = q_ref.shape
    heads = width // HEAD_DIM
    score_scale = HEAD_DIM ** (-0.5)
    part_rows = mem_rows // CHUNKS
    part_feats = block // CHUNKS
    far = far_to_near(z, n)
    near = far[::-1]

    own_slot = x * n + z
    loads = [
        pltpu.make_async_copy(src, dst, local_sem.at[i])
        for i, (src, dst) in enumerate(
            (
                (memory_ref, mem_all.at[own_slot]),
                (q_ref, q),
                (cot_ref, cot),
                (kw_ref, kw),
                (vw_ref, vw),
            )
        )
    ]
    for load in loads:
        load.start()
    length = len_ref[0]
    len_own[...] = jnp.full(len_own.shape, length.astype(jnp.float32), jnp.float32)

    barrier = pltpu.get_barrier_semaphore()
    pl.semaphore_signal(barrier, inc=1, device_id={"section": other}, device_id_type=MESH)
    for r in range(1, n_dp):
        peer = lax.rem(dp + r, n_dp)
        pl.semaphore_signal(barrier, inc=1, device_id={"dp": peer}, device_id_type=MESH)

    line_peers = 0
    for step in range(1, min(REACH, n - 1) + 1):

        @pl.when(z - step >= 0)
        def _():
            pl.semaphore_signal(barrier, inc=1, device_id={"mp": z - step}, device_id_type=MESH)

        @pl.when(z + step < n)
        def _():
            pl.semaphore_signal(barrier, inc=1, device_id={"mp": z + step}, device_id_type=MESH)

        line_peers += jnp.where(z - step >= 0, 1, 0) + jnp.where(z + step < n, 1, 0)
    pl.semaphore_wait(barrier, n_dp + line_peers)

    def distance(j):
        return jnp.where(j > z, j - z, z - j)

    def rows_of(c):
        return pl.ds(c * part_rows, part_rows)

    def send_block(src, slot, c, send_sem, device_id):
        return pltpu.make_async_remote_copy(
            src_ref=src,
            dst_ref=mem_all.at[slot, rows_of(c)],
            send_sem=send_sem,
            recv_sem=ag_recv.at[slot, c],
            device_id=device_id,
            device_id_type=MESH,
        )

    def to_line(k, c):
        return send_block(
            mem_all.at[own_slot, rows_of(c)], own_slot, c, ag_own_send.at[k, c], {"mp": near[k]}
        )

    def to_x(k, c):
        slot = x * n + near[k]
        return send_block(mem_all.at[slot, rows_of(c)], slot, c, ag_x_send.at[k, c], {"section": other})

    def relay(k, c):
        slot = x * n + near[k]
        dest = jnp.where(near[k] < z, z + 1, z - 1)
        return send_block(mem_all.at[slot, rows_of(c)], slot, c, ag_z_send.at[k, c], {"mp": dest})

    def relays(k):
        j = near[k]
        return (distance(j) >= REACH) & (((j < z) & (z < n - 1)) | ((j > z) & (z > 0)))

    def arrived(slot, c):
        send_block(mem_all.at[slot, rows_of(c)], slot, c, ag_x_send.at[0, c], {"section": other}).wait_recv()

    def reached(j):
        return distance(j) <= REACH

    def send_length(r):
        peer = lax.rem(dp + r, n_dp)
        return pltpu.make_async_remote_copy(
            src_ref=len_own,
            dst_ref=len_all.at[dp],
            send_sem=len_send.at[r],
            recv_sem=len_recv.at[dp],
            device_id={"dp": peer},
            device_id_type=MESH,
        )

    for r in range(1, n_dp):
        send_length(r).start()
    loads[0].wait()

    for c in range(CHUNKS):
        to_line(1, c).start()
        to_x(0, c).start()
    for k in range(2, n):
        for c in range(CHUNKS):

            @pl.when(reached(near[k]))
            def _():
                to_line(k, c).start()

    loads[1].wait()
    q_t[...] = q[...].T
    k_acc[...] = jnp.zeros_like(k_acc)
    v_acc[...] = jnp.zeros_like(v_acc)
    valid = (
        lax.broadcasted_iota(jnp.int32, (seq_rows, 1), 0) < length
    ).astype(jnp.float32)
    def weigh():
        total = len_own[...]
        for r in range(1, n_dp):
            peer = lax.rem(dp + r, n_dp)
            pltpu.make_async_remote_copy(
                src_ref=len_own,
                dst_ref=len_all.at[peer],
                send_sem=len_send.at[r],
                recv_sem=len_recv.at[peer],
                device_id={"dp": peer},
                device_id_type=MESH,
            ).wait_recv()
            total = total + len_all[peer]
        loss_weight = (float(n_dp * seq_rows) / total)[0:1, 0:1]
        loads[2].wait()
        weighted = (cot[...].astype(jnp.float32) * (valid * loss_weight)).astype(jnp.bfloat16)
        w[...] = weighted
        w_t[...] = weighted.T

    def project(slot):
        rows = pl.ds(pl.multiple_of(slot * block, block), block)
        mem_block = mem_all[slot]
        k_acc[...] += jnp.dot(mem_block, kw[rows, :], preferred_element_type=jnp.float32)
        v_acc[...] += jnp.dot(mem_block, vw[rows, :], preferred_element_type=jnp.float32)

    for k in range(1, n):
        for c in range(CHUNKS):
            arrived(x * n + near[k], c)

            @pl.when(relays(k))
            def _():
                relay(k, c).start()

            to_x(k, c).start()
        if k == 1:
            loads[3].wait()
            loads[4].wait()
        project(x * n + near[k - 1])
        if k == min(2, n - 1):
            weigh()

    @pl.loop(0, n + 1)
    def _(e):
        @pl.when(e > 0)
        def _():
            for c in range(CHUNKS):
                arrived(other * n + pick(near, e - 1), c)

        project(jnp.where(e == 0, x * n + near[n - 1], other * n + pick(near, e - 1)))

    last = (((1,), (1,)), ((), ()))

    @pl.loop(0, heads)
    def _(h):
        cols = pl.ds(pl.multiple_of(h * HEAD_DIM, HEAD_DIM), HEAD_DIM)
        key_h = k_acc[:, cols].astype(jnp.bfloat16)
        value_h = v_acc[:, cols].astype(jnp.bfloat16)
        scores = (
            lax.dot_general(q[:, cols], key_h, last, preferred_element_type=jnp.float32)
            * score_scale
        )
        prob_grad = lax.dot_general(w[:, cols], value_h, last, preferred_element_type=jnp.float32)
        top = jnp.max(scores, axis=-1, keepdims=True)
        powers = jnp.exp(scores - top)
        attention = powers * (1.0 / jnp.sum(powers, axis=-1, keepdims=True))
        attention_low = attention.astype(jnp.bfloat16)
        row_dot = jnp.sum(attention * prob_grad, axis=-1, keepdims=True)
        score_grad = (attention * (prob_grad - row_dot) * score_scale).astype(jnp.bfloat16)
        dv_t[cols, :] = jnp.dot(
            w_t[cols, :], attention_low, preferred_element_type=jnp.float32
        ).astype(jnp.bfloat16)
        dk_t[cols, :] = jnp.dot(
            q_t[cols, :], score_grad, preferred_element_type=jnp.float32
        ).astype(jnp.bfloat16)
        context = jnp.dot(attention_low, value_h, preferred_element_type=jnp.float32)
        ctx[:, cols] = (context * valid).astype(jnp.bfloat16)
    ctx_copy = pltpu.make_async_copy(ctx, ctx_out, local_sem.at[0])
    ctx_copy.start()

    def feats_of(c):
        return pl.ds(c * part_feats, part_feats)

    def sum_to_x(j, c):
        return pltpu.make_async_remote_copy(
            src_ref=xs.at[j, feats_of(c)],
            dst_ref=xr.at[j, feats_of(c)],
            send_sem=rs_x_send.at[j, c],
            recv_sem=rs_x_recv.at[j, c],
            device_id={"section": other},
            device_id_type=MESH,
        )

    def sum_along_z(j, c, slot):
        far_off = distance(j) > REACH
        step = jnp.where(j > z, z + 1, z - 1)
        return pltpu.make_async_remote_copy(
            src_ref=zs.at[j, feats_of(c)],
            dst_ref=zr.at[slot, feats_of(c)],
            send_sem=rs_z_send.at[j, c],
            recv_sem=rs_z_recv.at[slot, c],
            device_id={"mp": jnp.where(far_off, step, j)},
            device_id_type=MESH,
        )

    def grad_part(slot):
        rows = pl.ds(pl.multiple_of(slot * block, block), block)
        return jnp.dot(
            kw[rows, :], dk_t[...], preferred_element_type=jnp.float32
        ) + jnp.dot(vw[rows, :], dv_t[...], preferred_element_type=jnp.float32)

    @pl.loop(0, n)
    def _(k):
        j = pick(far, k)
        xs[j] = grad_part(other * n + j).astype(jnp.bfloat16)
        for c in range(CHUNKS):
            sum_to_x(j, c).start()

    def target_slot(j):
        return jnp.where(distance(j) > REACH, n + j, z)

    @pl.loop(0, n - 1)
    def _(k):
        j = pick(far, k)
        acc[j] = grad_part(x * n + j)
        has_source = (distance(j) >= REACH) & (
            ((j > z) & (z > 0)) | ((j < z) & (z < n - 1))
        )
        for c in range(CHUNKS):
            sum_to_x(j, c).wait_recv()
            acc[j, feats_of(c)] += xr[j, feats_of(c)].astype(jnp.float32)

            @pl.when(has_source)
            def _():
                sum_along_z(j, c, n + j).wait_recv()
                acc[j, feats_of(c)] += zr[n + j, feats_of(c)].astype(jnp.float32)

            zs[j, feats_of(c)] = acc[j, feats_of(c)].astype(jnp.bfloat16)
            sum_along_z(j, c, target_slot(j)).start()

    acc[z] = grad_part(own_slot)
    for c in range(CHUNKS):
        sum_to_x(z, c).wait_recv()
        grad_out[feats_of(c)] = acc[z, feats_of(c)] + xr[z, feats_of(c)].astype(jnp.float32)

        for k in range(1, n):

            @pl.when(reached(near[k]))
            def _():
                sum_along_z(near[k], c, near[k]).wait_recv()
                grad_out[feats_of(c)] += zr[near[k], feats_of(c)].astype(jnp.float32)

    for c in range(CHUNKS):
        for k in range(n):
            to_x(k, c).wait_send()
            sum_to_x(far[k], c).wait_send()
        for k in range(1, n):

            @pl.when(reached(near[k]))
            def _():
                to_line(k, c).wait_send()

            @pl.when(relays(k))
            def _():
                relay(k, c).wait_send()

        for k in range(n - 1):
            sum_along_z(far[k], c, target_slot(far[k])).wait_send()
    for r in range(1, n_dp):
        send_length(r).wait_send()
    ctx_copy.wait()


def fused(n, n_dp, memory, key_weight, value_weight, queries, cotangent, target_lengths):
    mem_rows, block = memory.shape[1:]
    feats, width = key_weight.shape[1:]
    seq_rows = queries.shape[2]
    low, full = jnp.bfloat16, jnp.float32
    vmem, sem = pltpu.VMEM, pltpu.SemaphoreType.DMA
    anywhere = pl.BlockSpec(memory_space=pl.ANY)
    context, grad = pl.pallas_call(
        functools.partial(fused_kernel, n, n_dp),
        out_shape=(
            jax.ShapeDtypeStruct((seq_rows, width), low),
            jax.ShapeDtypeStruct((block, mem_rows), full),
        ),
        in_specs=[pl.BlockSpec(memory_space=pltpu.SMEM)] + [anywhere] * 5,
        out_specs=(anywhere, pl.BlockSpec(memory_space=pltpu.VMEM)),
        scratch_shapes=[
            vmem((feats, width), low),
            vmem((feats, width), low),
            vmem((seq_rows, width), low),
            vmem((seq_rows, width), low),
            vmem((2 * n, mem_rows, block), low),
            vmem((mem_rows, width), full),
            vmem((mem_rows, width), full),
            vmem((width, seq_rows), low),
            vmem((seq_rows, width), low),
            vmem((width, seq_rows), low),
            vmem((seq_rows, width), low),
            vmem((width, mem_rows), low),
            vmem((width, mem_rows), low),
            vmem((n, block, mem_rows), low),
            vmem((n, block, mem_rows), low),
            vmem((n, block, mem_rows), full),
            vmem((n, block, mem_rows), low),
            vmem((2 * n, block, mem_rows), low),
            vmem((8, 128), full),
            vmem((n_dp, 8, 128), full),
            sem((5,)),
            sem((n, CHUNKS)),
            sem((n, CHUNKS)),
            sem((n, CHUNKS)),
            sem((2 * n, CHUNKS)),
            sem((n, CHUNKS)),
            sem((n, CHUNKS)),
            sem((n, CHUNKS)),
            sem((2 * n, CHUNKS)),
            sem((n_dp,)),
            sem((n_dp,)),
        ],
        compiler_params=pltpu.CompilerParams(
            collective_id=0, has_side_effects=True, vmem_limit_bytes=60 * 1024 * 1024
        ),
    )(
        target_lengths,
        memory[0],
        key_weight[0],
        value_weight[0],
        queries[0, 0],
        cotangent[0, 0],
    )
    context, grad = pl.pallas_call(
        finish_kernel,
        out_shape=(
            jax.ShapeDtypeStruct((seq_rows, width), low),
            jax.ShapeDtypeStruct((mem_rows, block), full),
        ),
        in_specs=[anywhere] * 2,
        out_specs=(anywhere, anywhere),
        scratch_shapes=[
            vmem((seq_rows, width), low),
            vmem((block, mem_rows), full),
            vmem((mem_rows, block), full),
            sem((4,)),
        ],
        compiler_params=pltpu.CompilerParams(vmem_limit_bytes=60 * 1024 * 1024),
    )(context, grad)
    return context[None, None], grad[None]


def on_device(memory, key_weight, value_weight, queries, cotangent, target_lengths):
    width = key_weight.shape[2]
    head_count = width // HEAD_DIM
    seq_rows = queries.shape[2]
    score_scale = HEAD_DIM ** (-0.5)
    mem_block = memory[0]
    mem_rows = mem_block.shape[0]
    full_memory = lax.all_gather(mem_block, ("section", "mp"), axis=1, tiled=True)
    token_total = lax.psum(target_lengths.astype(jnp.float32), "dp")
    slot_total = float(lax.axis_size("dp") * target_lengths.shape[0] * seq_rows)
    loss_weight = slot_total / token_total[0]
    valid = (jnp.arange(seq_rows, dtype=jnp.int32) < target_lengths[0]).astype(jnp.float32)
    layer_index = 0
    key_rows = jnp.dot(
        full_memory, key_weight[layer_index], preferred_element_type=jnp.float32
    ).astype(jnp.bfloat16)
    value_rows = jnp.dot(
        full_memory, value_weight[layer_index], preferred_element_type=jnp.float32
    ).astype(jnp.bfloat16)
    key_heads = key_rows.reshape(mem_rows, head_count, HEAD_DIM)
    value_heads = value_rows.reshape(mem_rows, head_count, HEAD_DIM)
    query_heads = queries[layer_index, 0].reshape(seq_rows, head_count, HEAD_DIM)
    scores = (
        jnp.einsum("thd,shd->hts", query_heads, key_heads, preferred_element_type=jnp.float32)
        * score_scale
    )
    attention = jax.nn.softmax(scores, axis=-1)
    attention_low = attention.astype(jnp.bfloat16)
    context = jnp.einsum(
        "hts,shd->thd", attention_low, value_heads, preferred_element_type=jnp.float32
    )
    context = (context * valid[:, None, None]).astype(jnp.bfloat16)
    contexts = [context.reshape(seq_rows, width)]
    weighted = cotangent[layer_index, 0].astype(jnp.float32) * (valid * loss_weight)[:, None]
    weighted = weighted.astype(jnp.bfloat16).reshape(seq_rows, head_count, HEAD_DIM)
    value_grad = jnp.einsum(
        "hts,thd->shd", attention_low, weighted, preferred_element_type=jnp.float32
    )
    value_grads = [value_grad.astype(jnp.bfloat16).reshape(mem_rows, width)]
    prob_grad = jnp.einsum(
        "thd,shd->hts", weighted, value_heads, preferred_element_type=jnp.float32
    )
    row_dot = jnp.sum(attention * prob_grad, axis=-1, keepdims=True)
    score_grad = (attention * (prob_grad - row_dot) * score_scale).astype(jnp.bfloat16)
    key_grad = jnp.einsum(
        "hts,thd->shd", score_grad, query_heads, preferred_element_type=jnp.float32
    )
    key_grads = [key_grad.astype(jnp.bfloat16).reshape(mem_rows, width)]
    contract_last = (((1,), (1,)), ((), ()))
    layer_index = 0
    key_part = key_weight[layer_index]
    value_part = value_weight[layer_index]
    running = lax.dot_general(
        key_part, key_grads[layer_index], contract_last, preferred_element_type=jnp.float32
    )
    running = running + lax.dot_general(
        value_part, value_grads[layer_index], contract_last, preferred_element_type=jnp.float32
    )
    section_part = lax.psum_scatter(
        running.astype(jnp.bfloat16), "section", scatter_dimension=0, tiled=True
    )
    own_part = lax.psum_scatter(section_part, "mp", scatter_dimension=0, tiled=True).astype(
        jnp.float32
    )
    own_grad = own_part.T
    context_out = jnp.stack(contexts, axis=0)[:, None]
    return (context_out, own_grad[None])


def solution(mesh):
    sections, n, n_dp = mesh.shape["section"], mesh.shape["mp"], mesh.shape["dp"]

    def per_device(memory, key_weight, value_weight, queries, cotangent, target_lengths):
        args = (memory, key_weight, value_weight, queries, cotangent, target_lengths)
        mem_rows, block = memory.shape[1:]
        if sections == 2 and n >= 2 and mem_rows % 128 == 0 and block % 128 == 0:
            return fused(n, n_dp, *args)
        return on_device(*args)

    return jax.shard_map(
        per_device,
        mesh=mesh,
        in_specs=(
            P("dp", None, ("section", "mp")),
            P("section", None, "mp"),
            P("section", None, "mp"),
            P("section", "dp", None, "mp"),
            P("section", "dp", None, "mp"),
            P("dp"),
        ),
        out_specs=(P("section", "dp", None, "mp"), P("dp", None, ("section", "mp"))),
        check_vma=False,
    )
```

```python
import functools

import jax
import jax.numpy as jnp
from jax import lax
from jax.experimental import pallas as pl
from jax.experimental.pallas import tpu as pltpu
from jax.sharding import PartitionSpec as P

HEAD_DIM = 256
CHUNKS = 2
REACH = 2
MESH = pl.DeviceIdType.MESH


def far_to_near(z, n):
    low, high, order = 0, n - 1, []
    for _ in range(n):
        take_low = (z - low) >= (high - z)
        order.append(jnp.where(take_low, low, high))
        low, high = jnp.where(take_low, low + 1, low), jnp.where(take_low, high, high - 1)
    return order


def pick(order, at):
    found = order[0]
    for i in range(1, len(order)):
        found = jnp.where(at == i, order[i], found)
    return found


def finish_kernel(ctx_ref, grad_ref, ctx_out, grad_out, ctx, grad, grad_t, sems):
    grad_load = pltpu.make_async_copy(grad_ref, grad, sems.at[0])
    ctx_load = pltpu.make_async_copy(ctx_ref, ctx, sems.at[1])
    grad_load.start()
    ctx_load.start()
    grad_load.wait()
    grad_t[...] = grad[...].T
    grad_store = pltpu.make_async_copy(grad_t, grad_out, sems.at[2])
    grad_store.start()
    ctx_load.wait()
    ctx_store = pltpu.make_async_copy(ctx, ctx_out, sems.at[3])
    ctx_store.start()
    grad_store.wait()
    ctx_store.wait()


def fused_kernel(
    n, n_dp,
    len_ref, memory_ref, kw_ref, vw_ref, q_ref, cot_ref,
    ctx_out, grad_out,
    kw, vw, q, cot, mem_all, k_acc, v_acc, q_t, w_t, ctx, probs, dk_t, dv_t,
    xs, xr, acc, zs, zr, len_own, len_all,
    local_sem, ag_own_send, ag_z_send, ag_x_send, ag_recv,
    rs_x_send, rs_x_recv, rs_z_send, rs_z_recv, len_send, len_recv,
):
    x = lax.axis_index("section")
    z = lax.axis_index("mp")
    dp = lax.axis_index("dp")
    other = 1 - x
    mem_rows, block = memory_ref.shape
    seq_rows, width = q_ref.shape
    heads = width // HEAD_DIM
    score_scale = HEAD_DIM ** (-0.5)
    part_rows = mem_rows // CHUNKS
    part_feats = block // CHUNKS
    far = far_to_near(z, n)
    near = far[::-1]

    own_slot = x * n + z
    loads = [
        pltpu.make_async_copy(src, dst, local_sem.at[i])
        for i, (src, dst) in enumerate(
            (
                (memory_ref, mem_all.at[own_slot]),
                (q_ref, q),
                (cot_ref, cot),
                (kw_ref, kw),
                (vw_ref, vw),
            )
        )
    ]
    for load in loads:
        load.start()
    length = len_ref[0]
    len_own[...] = jnp.full(len_own.shape, length.astype(jnp.float32), jnp.float32)

    barrier = pltpu.get_barrier_semaphore()
    pl.semaphore_signal(barrier, inc=1, device_id={"section": other}, device_id_type=MESH)
    for r in range(1, n_dp):
        peer = lax.rem(dp + r, n_dp)
        pl.semaphore_signal(barrier, inc=1, device_id={"dp": peer}, device_id_type=MESH)

    line_peers = 0
    for step in range(1, min(REACH, n - 1) + 1):

        @pl.when(z - step >= 0)
        def _():
            pl.semaphore_signal(barrier, inc=1, device_id={"mp": z - step}, device_id_type=MESH)

        @pl.when(z + step < n)
        def _():
            pl.semaphore_signal(barrier, inc=1, device_id={"mp": z + step}, device_id_type=MESH)

        line_peers += jnp.where(z - step >= 0, 1, 0) + jnp.where(z + step < n, 1, 0)
    pl.semaphore_wait(barrier, n_dp + line_peers)

    def distance(j):
        return jnp.where(j > z, j - z, z - j)

    def rows_of(c):
        return pl.ds(c * part_rows, part_rows)

    def send_block(src, slot, c, send_sem, device_id):
        return pltpu.make_async_remote_copy(
            src_ref=src,
            dst_ref=mem_all.at[slot, rows_of(c)],
            send_sem=send_sem,
            recv_sem=ag_recv.at[slot, c],
            device_id=device_id,
            device_id_type=MESH,
        )

    def to_line(k, c):
        return send_block(
            mem_all.at[own_slot, rows_of(c)], own_slot, c, ag_own_send.at[k, c], {"mp": near[k]}
        )

    def to_x(k, c):
        slot = x * n + near[k]
        return send_block(mem_all.at[slot, rows_of(c)], slot, c, ag_x_send.at[k, c], {"section": other})

    def relay(k, c):
        slot = x * n + near[k]
        dest = jnp.where(near[k] < z, z + 1, z - 1)
        return send_block(mem_all.at[slot, rows_of(c)], slot, c, ag_z_send.at[k, c], {"mp": dest})

    def relays(k):
        j = near[k]
        return (distance(j) >= REACH) & (((j < z) & (z < n - 1)) | ((j > z) & (z > 0)))

    def arrived(slot, c):
        send_block(mem_all.at[slot, rows_of(c)], slot, c, ag_x_send.at[0, c], {"section": other}).wait_recv()

    def reached(j):
        return distance(j) <= REACH

    def send_length(r):
        peer = lax.rem(dp + r, n_dp)
        return pltpu.make_async_remote_copy(
            src_ref=len_own,
            dst_ref=len_all.at[dp],
            send_sem=len_send.at[r],
            recv_sem=len_recv.at[dp],
            device_id={"dp": peer},
            device_id_type=MESH,
        )

    for r in range(1, n_dp):
        send_length(r).start()
    loads[0].wait()

    for c in range(CHUNKS):
        to_line(1, c).start()
        to_x(0, c).start()
    for k in range(2, n):
        for c in range(CHUNKS):

            @pl.when(reached(near[k]))
            def _():
                to_line(k, c).start()

    loads[1].wait()
    q_t[...] = q[...].T
    k_acc[...] = jnp.zeros_like(k_acc)
    v_acc[...] = jnp.zeros_like(v_acc)
    valid = (
        lax.broadcasted_iota(jnp.int32, (seq_rows, 1), 0) < length
    ).astype(jnp.float32)
    def weigh():
        total = len_own[...]
        for r in range(1, n_dp):
            peer = lax.rem(dp + r, n_dp)
            pltpu.make_async_remote_copy(
                src_ref=len_own,
                dst_ref=len_all.at[peer],
                send_sem=len_send.at[r],
                recv_sem=len_recv.at[peer],
                device_id={"dp": peer},
                device_id_type=MESH,
            ).wait_recv()
            total = total + len_all[peer]
        loss_weight = (float(n_dp * seq_rows) / total)[0:1, 0:1]
        loads[2].wait()
        weighted = (cot[...].astype(jnp.float32) * (valid * loss_weight)).astype(jnp.bfloat16)
        w_t[...] = weighted.T

    def project(slot):
        rows = pl.ds(pl.multiple_of(slot * block, block), block)
        mem_block = mem_all[slot]
        k_acc[...] += jnp.dot(mem_block, kw[rows, :], preferred_element_type=jnp.float32)
        v_acc[...] += jnp.dot(mem_block, vw[rows, :], preferred_element_type=jnp.float32)

    for k in range(1, n):
        for c in range(CHUNKS):
            arrived(x * n + near[k], c)

            @pl.when(relays(k))
            def _():
                relay(k, c).start()

            to_x(k, c).start()
        if k == 1:
            loads[3].wait()
            loads[4].wait()
        project(x * n + near[k - 1])
        if k == min(2, n - 1):
            weigh()

    @pl.loop(0, n + 1)
    def _(e):
        @pl.when(e > 0)
        def _():
            for c in range(CHUNKS):
                arrived(other * n + pick(near, e - 1), c)

        project(jnp.where(e == 0, x * n + near[n - 1], other * n + pick(near, e - 1)))

    last = (((1,), (1,)), ((), ()))

    @pl.loop(0, heads)
    def _(h):
        cols = pl.ds(pl.multiple_of(h * HEAD_DIM, HEAD_DIM), HEAD_DIM)
        key_h = k_acc[:, cols].astype(jnp.bfloat16)
        value_h = v_acc[:, cols].astype(jnp.bfloat16)
        scores = (
            jnp.dot(key_h, q_t[cols, :], preferred_element_type=jnp.float32) * score_scale
        )
        prob_grad = jnp.dot(value_h, w_t[cols, :], preferred_element_type=jnp.float32)
        top = jnp.max(scores, axis=0, keepdims=True)
        powers = jnp.exp(scores - top)
        attention = powers * (1.0 / jnp.sum(powers, axis=0, keepdims=True))
        attention_low = attention.astype(jnp.bfloat16)
        probs[h] = attention_low
        column_dot = jnp.sum(attention * prob_grad, axis=0, keepdims=True)
        score_grad = (attention * (prob_grad - column_dot) * score_scale).astype(jnp.bfloat16)
        dv_t[cols, :] = lax.dot_general(
            w_t[cols, :], attention_low, last, preferred_element_type=jnp.float32
        ).astype(jnp.bfloat16)
        dk_t[cols, :] = lax.dot_general(
            q_t[cols, :], score_grad, last, preferred_element_type=jnp.float32
        ).astype(jnp.bfloat16)

    def feats_of(c):
        return pl.ds(c * part_feats, part_feats)

    def sum_to_x(j, c):
        return pltpu.make_async_remote_copy(
            src_ref=xs.at[j, feats_of(c)],
            dst_ref=xr.at[j, feats_of(c)],
            send_sem=rs_x_send.at[j, c],
            recv_sem=rs_x_recv.at[j, c],
            device_id={"section": other},
            device_id_type=MESH,
        )

    def sum_along_z(j, c, slot):
        far_off = distance(j) > REACH
        step = jnp.where(j > z, z + 1, z - 1)
        return pltpu.make_async_remote_copy(
            src_ref=zs.at[j, feats_of(c)],
            dst_ref=zr.at[slot, feats_of(c)],
            send_sem=rs_z_send.at[j, c],
            recv_sem=rs_z_recv.at[slot, c],
            device_id={"mp": jnp.where(far_off, step, j)},
            device_id_type=MESH,
        )

    def grad_part(slot):
        rows = pl.ds(pl.multiple_of(slot * block, block), block)
        return jnp.dot(
            kw[rows, :], dk_t[...], preferred_element_type=jnp.float32
        ) + jnp.dot(vw[rows, :], dv_t[...], preferred_element_type=jnp.float32)

    @pl.loop(0, n)
    def _(k):
        j = pick(far, k)
        xs[j] = grad_part(other * n + j).astype(jnp.bfloat16)
        for c in range(CHUNKS):
            sum_to_x(j, c).start()

    def target_slot(j):
        return jnp.where(distance(j) > REACH, n + j, z)

    @pl.loop(0, n - 1)
    def _(k):
        j = pick(far, k)
        acc[j] = grad_part(x * n + j)
        has_source = (distance(j) >= REACH) & (
            ((j > z) & (z > 0)) | ((j < z) & (z < n - 1))
        )
        for c in range(CHUNKS):
            sum_to_x(j, c).wait_recv()
            acc[j, feats_of(c)] += xr[j, feats_of(c)].astype(jnp.float32)

            @pl.when(has_source)
            def _():
                sum_along_z(j, c, n + j).wait_recv()
                acc[j, feats_of(c)] += zr[n + j, feats_of(c)].astype(jnp.float32)

            zs[j, feats_of(c)] = acc[j, feats_of(c)].astype(jnp.bfloat16)
            sum_along_z(j, c, target_slot(j)).start()

    @pl.loop(0, heads)
    def _(h):
        cols = pl.ds(pl.multiple_of(h * HEAD_DIM, HEAD_DIM), HEAD_DIM)
        context = lax.dot_general(
            probs[h],
            v_acc[:, cols].astype(jnp.bfloat16),
            (((0,), (0,)), ((), ())),
            preferred_element_type=jnp.float32,
        )
        ctx[:, cols] = (context * valid).astype(jnp.bfloat16)

    ctx_copy = pltpu.make_async_copy(ctx, ctx_out, local_sem.at[0])
    ctx_copy.start()
    acc[z] = grad_part(own_slot)
    for c in range(CHUNKS):
        sum_to_x(z, c).wait_recv()
        grad_out[feats_of(c)] = acc[z, feats_of(c)] + xr[z, feats_of(c)].astype(jnp.float32)

        for k in range(1, n):

            @pl.when(reached(near[k]))
            def _():
                sum_along_z(near[k], c, near[k]).wait_recv()
                grad_out[feats_of(c)] += zr[near[k], feats_of(c)].astype(jnp.float32)

    for c in range(CHUNKS):
        for k in range(n):
            to_x(k, c).wait_send()
            sum_to_x(far[k], c).wait_send()
        for k in range(1, n):

            @pl.when(reached(near[k]))
            def _():
                to_line(k, c).wait_send()

            @pl.when(relays(k))
            def _():
                relay(k, c).wait_send()

        for k in range(n - 1):
            sum_along_z(far[k], c, target_slot(far[k])).wait_send()
    for r in range(1, n_dp):
        send_length(r).wait_send()
    ctx_copy.wait()


def fused(n, n_dp, memory, key_weight, value_weight, queries, cotangent, target_lengths):
    mem_rows, block = memory.shape[1:]
    feats, width = key_weight.shape[1:]
    seq_rows = queries.shape[2]
    low, full = jnp.bfloat16, jnp.float32
    vmem, sem = pltpu.VMEM, pltpu.SemaphoreType.DMA
    anywhere = pl.BlockSpec(memory_space=pl.ANY)
    context, grad = pl.pallas_call(
        functools.partial(fused_kernel, n, n_dp),
        out_shape=(
            jax.ShapeDtypeStruct((seq_rows, width), low),
            jax.ShapeDtypeStruct((block, mem_rows), full),
        ),
        in_specs=[pl.BlockSpec(memory_space=pltpu.SMEM)] + [anywhere] * 5,
        out_specs=(anywhere, pl.BlockSpec(memory_space=pltpu.VMEM)),
        scratch_shapes=[
            vmem((feats, width), low),
            vmem((feats, width), low),
            vmem((seq_rows, width), low),
            vmem((seq_rows, width), low),
            vmem((2 * n, mem_rows, block), low),
            vmem((mem_rows, width), full),
            vmem((mem_rows, width), full),
            vmem((width, seq_rows), low),
            vmem((width, seq_rows), low),
            vmem((seq_rows, width), low),
            vmem((width // HEAD_DIM, mem_rows, seq_rows), low),
            vmem((width, mem_rows), low),
            vmem((width, mem_rows), low),
            vmem((n, block, mem_rows), low),
            vmem((n, block, mem_rows), low),
            vmem((n, block, mem_rows), full),
            vmem((n, block, mem_rows), low),
            vmem((2 * n, block, mem_rows), low),
            vmem((8, 128), full),
            vmem((n_dp, 8, 128), full),
            sem((5,)),
            sem((n, CHUNKS)),
            sem((n, CHUNKS)),
            sem((n, CHUNKS)),
            sem((2 * n, CHUNKS)),
            sem((n, CHUNKS)),
            sem((n, CHUNKS)),
            sem((n, CHUNKS)),
            sem((2 * n, CHUNKS)),
            sem((n_dp,)),
            sem((n_dp,)),
        ],
        compiler_params=pltpu.CompilerParams(
            collective_id=0, has_side_effects=True, vmem_limit_bytes=60 * 1024 * 1024
        ),
    )(
        target_lengths,
        memory[0],
        key_weight[0],
        value_weight[0],
        queries[0, 0],
        cotangent[0, 0],
    )
    context, grad = pl.pallas_call(
        finish_kernel,
        out_shape=(
            jax.ShapeDtypeStruct((seq_rows, width), low),
            jax.ShapeDtypeStruct((mem_rows, block), full),
        ),
        in_specs=[anywhere] * 2,
        out_specs=(anywhere, anywhere),
        scratch_shapes=[
            vmem((seq_rows, width), low),
            vmem((block, mem_rows), full),
            vmem((mem_rows, block), full),
            sem((4,)),
        ],
        compiler_params=pltpu.CompilerParams(vmem_limit_bytes=60 * 1024 * 1024),
    )(context, grad)
    return context[None, None], grad[None]


def on_device(memory, key_weight, value_weight, queries, cotangent, target_lengths):
    width = key_weight.shape[2]
    head_count = width // HEAD_DIM
    seq_rows = queries.shape[2]
    score_scale = HEAD_DIM ** (-0.5)
    mem_block = memory[0]
    mem_rows = mem_block.shape[0]
    full_memory = lax.all_gather(mem_block, ("section", "mp"), axis=1, tiled=True)
    token_total = lax.psum(target_lengths.astype(jnp.float32), "dp")
    slot_total = float(lax.axis_size("dp") * target_lengths.shape[0] * seq_rows)
    loss_weight = slot_total / token_total[0]
    valid = (jnp.arange(seq_rows, dtype=jnp.int32) < target_lengths[0]).astype(jnp.float32)
    layer_index = 0
    key_rows = jnp.dot(
        full_memory, key_weight[layer_index], preferred_element_type=jnp.float32
    ).astype(jnp.bfloat16)
    value_rows = jnp.dot(
        full_memory, value_weight[layer_index], preferred_element_type=jnp.float32
    ).astype(jnp.bfloat16)
    key_heads = key_rows.reshape(mem_rows, head_count, HEAD_DIM)
    value_heads = value_rows.reshape(mem_rows, head_count, HEAD_DIM)
    query_heads = queries[layer_index, 0].reshape(seq_rows, head_count, HEAD_DIM)
    scores = (
        jnp.einsum("thd,shd->hts", query_heads, key_heads, preferred_element_type=jnp.float32)
        * score_scale
    )
    attention = jax.nn.softmax(scores, axis=-1)
    attention_low = attention.astype(jnp.bfloat16)
    context = jnp.einsum(
        "hts,shd->thd", attention_low, value_heads, preferred_element_type=jnp.float32
    )
    context = (context * valid[:, None, None]).astype(jnp.bfloat16)
    contexts = [context.reshape(seq_rows, width)]
    weighted = cotangent[layer_index, 0].astype(jnp.float32) * (valid * loss_weight)[:, None]
    weighted = weighted.astype(jnp.bfloat16).reshape(seq_rows, head_count, HEAD_DIM)
    value_grad = jnp.einsum(
        "hts,thd->shd", attention_low, weighted, preferred_element_type=jnp.float32
    )
    value_grads = [value_grad.astype(jnp.bfloat16).reshape(mem_rows, width)]
    prob_grad = jnp.einsum(
        "thd,shd->hts", weighted, value_heads, preferred_element_type=jnp.float32
    )
    row_dot = jnp.sum(attention * prob_grad, axis=-1, keepdims=True)
    score_grad = (attention * (prob_grad - row_dot) * score_scale).astype(jnp.bfloat16)
    key_grad = jnp.einsum(
        "hts,thd->shd", score_grad, query_heads, preferred_element_type=jnp.float32
    )
    key_grads = [key_grad.astype(jnp.bfloat16).reshape(mem_rows, width)]
    contract_last = (((1,), (1,)), ((), ()))
    layer_index = 0
    key_part = key_weight[layer_index]
    value_part = value_weight[layer_index]
    running = lax.dot_general(
        key_part, key_grads[layer_index], contract_last, preferred_element_type=jnp.float32
    )
    running = running + lax.dot_general(
        value_part, value_grads[layer_index], contract_last, preferred_element_type=jnp.float32
    )
    section_part = lax.psum_scatter(
        running.astype(jnp.bfloat16), "section", scatter_dimension=0, tiled=True
    )
    own_part = lax.psum_scatter(section_part, "mp", scatter_dimension=0, tiled=True).astype(
        jnp.float32
    )
    own_grad = own_part.T
    context_out = jnp.stack(contexts, axis=0)[:, None]
    return (context_out, own_grad[None])


def solution(mesh):
    sections, n, n_dp = mesh.shape["section"], mesh.shape["mp"], mesh.shape["dp"]

    def per_device(memory, key_weight, value_weight, queries, cotangent, target_lengths):
        args = (memory, key_weight, value_weight, queries, cotangent, target_lengths)
        mem_rows, block = memory.shape[1:]
        if sections == 2 and n >= 2 and mem_rows % 128 == 0 and block % 128 == 0:
            return fused(n, n_dp, *args)
        return on_device(*args)

    return jax.shard_map(
        per_device,
        mesh=mesh,
        in_specs=(
            P("dp", None, ("section", "mp")),
            P("section", None, "mp"),
            P("section", None, "mp"),
            P("section", "dp", None, "mp"),
            P("section", "dp", None, "mp"),
            P("dp"),
        ),
        out_specs=(P("section", "dp", None, "mp"), P("dp", None, ("section", "mp"))),
        check_vma=False,
    )
```
